256 devices in a mesh: seq: 16 (over z, y_lo), head: 8 (over x, y_hi), rows: 2 (over core).
Axes of the slice: x: 4, y: 4 (y_hi: 2, y_lo: 2; y = y_hi * 2 + y_lo), z: 8, core: 2. Of those that a mesh axis runs over, the one named last changes fastest.
Arguments:
- queries: bfloat16 [512, 64, 128], P(('rows', 'seq'), 'head'), may hold values from -15 to 15
- row_adapter: int32 [512], P(('rows', 'seq')), may hold values from 0 to 63
- doc_keys: bfloat16 [65536, 8, 128], P('seq', 'head'), may hold values from -6 to 6
- doc_values: bfloat16 [65536, 8, 128], P('seq', 'head'), may hold values from -6 to 6
- patch_keys: bfloat16 [256, 128, 8, 128], P('seq', None, 'head'), may hold values from -8 to 8
- patch_values: bfloat16 [256, 128, 8, 128], P('seq', None, 'head'), may hold values from -6 to 6
- patch_block: int32 [256], replicated, may hold values from 0 to 511, as said below
- patch_slot: int32 [256], replicated, may hold values from 0 to 255, each once
- out_weight: bfloat16 [8192, 8192], P('head', 'seq'), may hold values from -0.0625 to 0.0625
Outputs:
- mixed: float32 [512, 8192], P(('rows', 'head'), 'seq')
The draws below stay inside these ranges and needn't reach their ends.
Inputs may be any that keep to these rules, and one draw needn't show every extreme that they name: `patch_block`: the 4 entries of one adapter name different blocks. `patch_slot`: each slot is named by one entry.
All inputs are finite; a program needn't handle non-finite values.
Results may differ from the reference program's by a relative error of at most 0.004.
Values may be sent and summed in bfloat16 or wider, within the bound.
No kernel may reach another device: no remote copies, remote signals or barrier semaphores. Data moves between devices by JAX's collectives and lax.ppermute only.
A program may use at most 64 MiB of HBM per device.

```python
import math
import jax
import jax.numpy as jnp
import numpy as np
from jax import lax

D = 8192
QH = 64
KVH = 8
HD = 128
DOC_DEV = 4096
BLK = 128
ADAPTERS = 64
PATCHES = 4
ROWS = 512
DOC = 65536
NBLK = 512
SLOTS = 256
N_SEQ = 16


def draw_queries(key, part):
    key = jax.random.fold_in(key, 11)
    first = jax.random.fold_in(key, 0)
    shape = (ROWS, QH, HD)
    values = jnp.clip(3.0 * jax.random.normal(first, shape, jnp.float32), -15.0, 15.0)
    return values.astype(jnp.bfloat16)


def draw_doc_keys(key, part):
    key = jax.random.fold_in(key, 17)
    first = jax.random.fold_in(key, 0)
    shape = (DOC, KVH, HD)
    base = jax.random.normal(first, shape, jnp.float32)
    values = jnp.clip(base, -6.0, 6.0)
    return values.astype(jnp.bfloat16)


def draw_patch_block(key, part):
    key = jax.random.fold_in(key, 23)
    first, second = jax.random.split(key)
    columns = jnp.arange(NBLK, dtype=jnp.int32)
    scores = jax.random.randint(first, (ADAPTERS, NBLK), 0, 4096, dtype=jnp.int32) * NBLK + columns[None, :]
    chosen = jax.random.randint(second, (), 0, ADAPTERS, dtype=jnp.int32)
    ends = jnp.logical_or(columns == 0, columns == NBLK - 1)
    planted = jnp.logical_and((jnp.arange(ADAPTERS, dtype=jnp.int32) == chosen)[:, None], ends[None, :])
    scores = jnp.where(planted, 4096 * NBLK + columns[None, :], scores)
    _, picked = lax.top_k(scores, PATCHES)
    return picked.astype(jnp.int32).reshape(SLOTS)


def plant(values, rng, least, high):
    longest = values.shape.index(max(values.shape))
    spots = []
    for shift in (0, 1):
        where = [jax.random.randint(jax.random.fold_in(rng, axis), (), 0, length) for axis, length in enumerate(values.shape)]
        where[longest] = (where[longest] + shift) % values.shape[longest]
        spots.append(tuple(where))
    return values.at[spots[0]].set(least).at[spots[1]].set(high)


def block_levels(own_key, dims, pieces, low, largest):
    def one(dim, shards_of):
        steps = jax.random.uniform(jax.random.fold_in(jax.random.fold_in(own_key, 6), dim), (shards_of,), jnp.float32, low / len(pieces), largest / len(pieces))
        return jnp.repeat(jnp.exp(steps), dims[dim] // shards_of).reshape((-1,) + (1,) * (len(dims) - dim - 1))

    gain = one(*pieces[0])
    for cut in pieces[1:]:
        gain = gain * one(*cut)
    return gain


def cumulative_ranks(count, lean):
    portions = [(1 << 20) // math.isqrt(standing ** lean) + 1 for standing in range(1, count + 1)]
    scale = 1 + sum(portions) // (1 << 30)
    return np.cumsum(np.array([max(1, weight // scale) for weight in portions]))


def ranked(key, extent, count, lean):
    table = cumulative_ranks(count, lean)
    ticket = jax.random.randint(jax.random.fold_in(key, 1), extent, 0, int(table[count - 1]))
    standing = jnp.searchsorted(jnp.asarray(table, jnp.int32), ticket, side="right")
    return jax.random.permutation(jax.random.fold_in(key, 2), count)[standing].astype(jnp.int32)


def bell_draw(rng, dims, deviation, most, cuts=(), held_as=jnp.bfloat16):
    drawn = deviation * jax.random.normal(rng, dims, jnp.float32)
    if cuts:
        drawn = drawn * block_levels(rng, dims, cuts, -0.22, 0.18)
    return jnp.clip(drawn, -most, most).astype(held_as)


def setup_inputs(seed: int = 0) -> dict:
    arg_keys = jax.random.split(jax.random.key(seed), 10)
    return {
        "queries": draw_queries(jax.random.fold_in(arg_keys[9], 71), 0),
        "row_adapter": plant(ranked(arg_keys[1], (ROWS,), ADAPTERS, 2), jax.random.fold_in(arg_keys[1], 3), 0, ADAPTERS - 1).astype(jnp.int32),
        "doc_keys": draw_doc_keys(jax.random.fold_in(arg_keys[9], 71), 0),
        "doc_values": bell_draw(arg_keys[3], (DOC, KVH, HD), 1.0, 6.0, ((0, 16), (1, 8))),
        "patch_keys": bell_draw(arg_keys[4], (SLOTS, BLK, KVH, HD), 1.4, 8.0, ((0, 16), (2, 8))),
        "patch_values": bell_draw(arg_keys[5], (SLOTS, BLK, KVH, HD), 1.0, 6.0, ((0, 16), (2, 8))),
        "patch_block": draw_patch_block(jax.random.fold_in(arg_keys[9], 71), 0),
        "patch_slot": jax.random.permutation(arg_keys[7], SLOTS).astype(jnp.int32),
        "out_weight": bell_draw(arg_keys[8], (QH * HD, D), (QH * HD) ** -0.5, 0.0625, ((0, 8), (1, 16))),
    }


masked_score = -1e30


def reference(queries, row_adapter, doc_keys, doc_values, patch_keys, patch_values, patch_block, patch_slot, out_weight):
    group = QH // KVH
    scale = HD ** -0.5
    row_blocks = patch_block.reshape(ADAPTERS, PATCHES)[row_adapter]
    row_slots = patch_slot.reshape(ADAPTERS, PATCHES)[row_adapter]
    per_span = DOC_DEV // BLK
    grouped = queries.astype(jnp.float32).reshape(ROWS, KVH, group, HD).transpose(1, 0, 2, 3)
    dkeys = doc_keys.transpose(1, 0, 2).reshape(KVH, N_SEQ, DOC_DEV, HD)
    dvalues = doc_values.transpose(1, 0, 2).reshape(KVH, N_SEQ, DOC_DEV, HD)
    pkeys = patch_keys.transpose(2, 0, 1, 3)
    pvalues = patch_values.transpose(2, 0, 1, 3)
    span_ids = jnp.arange(N_SEQ, dtype=jnp.int32)

    def one_head(items):
        query, keys, values, store_keys, store_values = items
        row_keys = store_keys[row_slots].astype(jnp.float32)
        row_values = store_values[row_slots].astype(jnp.float32)
        patch_scores = jnp.einsum("rgd,rpbd->rgpb", query, row_keys) * scale

        def scores_of(index, kblock):
            scores = jnp.einsum("rgd,td->rgt", query, kblock.astype(jnp.float32)) * scale
            block_ids = index * per_span + jnp.arange(per_span, dtype=jnp.int32)
            hidden_blocks = jnp.any(row_blocks[:, :, None] == block_ids[None, None, :], axis=1)
            scores = scores.reshape(ROWS, group, per_span, BLK)
            return jnp.where(jnp.logical_not(hidden_blocks)[:, None, :, None], scores, masked_score)

        def max_step(running, item):
            index, kblock = item
            return jnp.maximum(running, jnp.max(scores_of(index, kblock), axis=(2, 3))), None

        peak, _ = lax.scan(max_step, jnp.max(patch_scores, axis=(2, 3)), (span_ids, keys))
        patch_weights = jnp.exp(patch_scores - peak[:, :, None, None]).astype(jnp.bfloat16)
        patch_weights = lax.optimization_barrier(patch_weights).astype(jnp.float32)
        start = (jnp.sum(patch_weights, axis=(2, 3)), jnp.einsum("rgpb,rpbd->rgd", patch_weights, row_values))

        def sum_step(carry, item):
            total, accum = carry
            index, kblock, vblock = item
            weights = jnp.exp(scores_of(index, kblock) - peak[:, :, None, None]).astype(jnp.bfloat16)
            weights = lax.optimization_barrier(weights).astype(jnp.float32)
            total = total + jnp.sum(weights, axis=(2, 3))
            accum = accum + jnp.einsum("rgsb,sbd->rgd", weights, vblock.astype(jnp.float32).reshape(per_span, BLK, HD))
            return (total, accum), None

        (total, accum), _ = lax.scan(sum_step, start, (span_ids, keys, values))
        return accum / total[:, :, None]

    attended = lax.map(one_head, (grouped, dkeys, dvalues, pkeys, pvalues))
    attended = attended.transpose(1, 0, 2, 3).reshape(ROWS, QH * HD).astype(jnp.bfloat16)
    return jnp.dot(attended, out_weight, preferred_element_type=jnp.float32)
```

```python
import functools
import math

import jax
import jax.numpy as jnp
from jax import lax
from jax.experimental import pallas as pl
from jax.experimental.pallas import tpu as pltpu
from jax.sharding import PartitionSpec as P

BLK = 128
ADAPTERS = 64
PATCHES = 4
HD = 128
RATE = math.log2(math.e) / math.sqrt(HD)
HIDDEN = -1e30
TAIL = 16
SPAN = 512
VMEM = 24 * 2**20


def pack(query_ref, adapter_ref, out_ref):
    rows, heads, width = query_ref.shape
    query = query_ref[...].astype(jnp.float32)
    line = lax.broadcasted_iota(jnp.int32, (rows, width), 0)
    lane = lax.broadcasted_iota(jnp.int32, (rows, width), 1)
    onehot = jnp.zeros((rows, width), jnp.float32)
    for r in range(rows):
        onehot = jnp.where((line == r) & (lane == adapter_ref[r]), 1.0, onehot)
    lines = [query[:, h, :] for h in range(heads)] + [onehot]
    message = jnp.concatenate(lines, 0).astype(jnp.bfloat16)
    for i in range(out_ref.shape[0]):
        out_ref[i] = message


def store_part(out_ref, i, mean, logsum):
    lines = mean.shape[0]
    line = lax.broadcasted_iota(jnp.int32, (TAIL, lines), 0)
    out_ref[i, :lines, :] = mean.astype(jnp.bfloat16)
    flat = jnp.transpose(logsum)[:TAIL, :]
    first = flat.astype(jnp.bfloat16).astype(jnp.float32)
    second = (flat - first).astype(jnp.bfloat16).astype(jnp.float32)
    third = flat - first - second
    tail = jnp.where(
        line == 0, first, jnp.where(line == 1, second, jnp.where(line == 2, third, 0.0))
    )
    out_ref[i, lines:, :] = tail.astype(jnp.bfloat16)


def local_attention(msg_ref, keys_ref, values_ref):
    count = msg_ref.shape[0]
    lines = msg_ref.shape[1] - TAIL
    heads = lines // TAIL
    tokens = keys_ref.shape[0]
    parts = []
    for i in range(count):
        onehot = msg_ref[i, lines:, :]
        parts.append(
            jnp.concatenate(
                [msg_ref[i, :lines, :], jnp.concatenate([onehot] * heads, 0)], 1
            )
        )
    query = jnp.concatenate(parts, 0)
    peak = accum = None
    for start in range(0, tokens, SPAN):
        scores = lax.dot_general(
            query,
            keys_ref[start : start + SPAN, :],
            (((1,), (1,)), ((), ())),
            preferred_element_type=jnp.float32,
        )
        top = jnp.max(scores, axis=1, keepdims=True)
        if accum is not None:
            top = jnp.maximum(peak, top)
        weights = jnp.exp2((scores - top) * RATE).astype(jnp.bfloat16)
        added = jnp.dot(
            weights, values_ref[start : start + SPAN, :], preferred_element_type=jnp.float32
        )
        accum = added if accum is None else accum * jnp.exp2((peak - top) * RATE) + added
        peak = top
    total = accum[:, HD:]
    mean = accum[:, :HD] / total
    return mean, peak * RATE + jnp.log2(total)


def attend_sent(msg_ref, keys_ref, values_ref, out_ref):
    mean, logsum = local_attention(msg_ref, keys_ref, values_ref)
    lines = msg_ref.shape[1] - TAIL
    for i in range(msg_ref.shape[0]):
        store_part(
            out_ref, i, mean[i * lines : (i + 1) * lines], logsum[i * lines : (i + 1) * lines]
        )


def attend_kept(msg_ref, keys_ref, values_ref, mean_ref, logsum_ref):
    mean, logsum = local_attention(msg_ref, keys_ref, values_ref)
    lines = msg_ref.shape[1] - TAIL
    for i in range(msg_ref.shape[0]):
        mean_ref[i] = mean[i * lines : (i + 1) * lines]
        logsum_ref[i] = logsum[i * lines : (i + 1) * lines]


def columns(flat, lines):
    count = flat.shape[0]
    return jnp.transpose(
        jnp.concatenate([flat, jnp.zeros((lines - count, lines), jnp.float32)], 0)
    )


def merge(mean_ref, logsum_ref, two_ref, out_ref):
    count = two_ref.shape[0]
    lines = two_ref.shape[1] - TAIL
    others = columns(jnp.sum(two_ref[:, lines:, :].astype(jnp.float32), axis=1), lines)
    for i in range(count):
        one, two = logsum_ref[i], others[:, i : i + 1]
        top = jnp.maximum(one, two)
        first, second = jnp.exp2(one - top), jnp.exp2(two - top)
        both = first + second
        mean = (mean_ref[i] * first + two_ref[i, :lines, :].astype(jnp.float32) * second) / both
        store_part(out_ref, i, mean, top + jnp.log2(both))


def combine(parts_ref, out_ref):
    count = parts_ref.shape[0]
    lines = parts_ref.shape[1] - TAIL
    heads = lines // TAIL
    logsum = jnp.sum(parts_ref[:, lines:, :].astype(jnp.float32), axis=1)
    share = jnp.exp2(logsum - jnp.max(logsum, axis=0, keepdims=True))
    share = columns(share / jnp.sum(share, axis=0, keepdims=True), lines)
    mixed = None
    for i in range(count):
        term = parts_ref[i, :lines, :].astype(jnp.float32) * share[:, i : i + 1]
        mixed = term if mixed is None else mixed + term
    attended = mixed.astype(jnp.bfloat16)
    wide = jnp.concatenate([attended[h * TAIL : (h + 1) * TAIL] for h in range(heads)], 1)
    for i in range(out_ref.shape[0]):
        out_ref[i] = wide


def project(side_ref, rows_ref, own_ref, other_ref, out_ref):
    side = side_ref[0]
    count, own = rows_ref.shape[0], rows_ref.shape[1]
    rows = jnp.concatenate([rows_ref[i] for i in range(count)], 0)
    for weight_ref, place in ((own_ref, 1 - side), (other_ref, side)):
        product = jnp.dot(rows, weight_ref[...], preferred_element_type=jnp.float32)
        product = product.astype(jnp.bfloat16)
        for i in range(count):
            out_ref[i, place] = product[i * own : (i + 1) * own]


def per_device(
    queries,
    row_adapter,
    doc_keys,
    doc_values,
    patch_keys,
    patch_values,
    patch_block,
    patch_slot,
    out_weight,
):
    seqs = lax.axis_size("seq")
    groups = lax.axis_size("head")
    pairs = seqs // 2
    own, heads, width = queries.shape
    lines = own * heads
    seq_index = lax.axis_index("seq")
    side = lax.rem(seq_index, 2)
    adapter_ids = jnp.arange(HD, dtype=jnp.int32)
    levels = [[2 * level + at for level in range(pairs)] for at in range(2)]
    corners = [
        [head * seqs + 2 * level + at for head in range(groups) for at in (1, 0)]
        for level in range(pairs)
    ]

    def partner(array):
        return lax.ppermute(array, "seq", [(i, i ^ 1) for i in range(seqs)])

    def along_levels(array):
        return lax.all_to_all(array, "seq", 0, 0, tiled=True, axis_index_groups=levels)

    vmem = pltpu.CompilerParams(vmem_limit_bytes=VMEM)
    small = pltpu.CompilerParams(vmem_limit_bytes=16 * 2**20)
    part_shape = jax.ShapeDtypeStruct((pairs, lines + TAIL, width), jnp.bfloat16)

    message = pl.pallas_call(
        pack,
        in_specs=[
            pl.BlockSpec(memory_space=pltpu.VMEM),
            pl.BlockSpec(memory_space=pltpu.SMEM),
        ],
        out_shape=part_shape,
        compiler_params=small,
        name="pack",
    )(queries, row_adapter)
    with jax.named_scope("gather_queries"):
        near = along_levels(message)
        far = partner(near)
    with jax.named_scope("local_tokens"):
        doc_len = doc_keys.shape[0]
        blocks_here = doc_len // BLK
        slots_here = patch_keys.shape[0]
        block_ids = seq_index * blocks_here + jnp.arange(blocks_here, dtype=jnp.int32)
        replaced = jnp.pad(
            patch_block.reshape(ADAPTERS, PATCHES),
            ((0, HD - ADAPTERS), (0, 0)),
            constant_values=-1,
        )
        hides = jnp.any(block_ids[:, None, None] == replaced[None, :, :], axis=2)
        slot_ids = seq_index * slots_here + jnp.arange(slots_here, dtype=jnp.int32)
        entry_owner = jnp.arange(patch_slot.shape[0], dtype=jnp.int32) // PATCHES
        slot_adapter = jnp.sum(
            jnp.where(slot_ids[:, None] == patch_slot[None, :], entry_owner[None, :], 0), axis=1
        )
        hides = jnp.concatenate([hides, slot_adapter[:, None] != adapter_ids[None, :]], 0)
        bars = jnp.where(hides, HIDDEN, 0.0).astype(jnp.bfloat16)
        bars = jnp.broadcast_to(bars[:, None, :], (blocks_here + slots_here, BLK, HD))
        tokens = doc_len + slots_here * BLK
        keys = jnp.concatenate(
            [doc_keys.reshape(doc_len, width), patch_keys.reshape(slots_here * BLK, width)], 0
        )
        keys = jnp.concatenate([keys, bars.reshape(tokens, HD)], 1)
        values = jnp.concatenate(
            [doc_values.reshape(doc_len, width), patch_values.reshape(slots_here * BLK, width)], 0
        )
        values = jnp.concatenate([values, jnp.ones((tokens, HD), jnp.bfloat16)], 1)

    kept_shape = jax.ShapeDtypeStruct((pairs, lines, width), jnp.float32)

    def attend_lines(body, out_shape):
        return pl.pallas_call(
            body,
            out_shape=out_shape,
            compiler_params=vmem,
            cost_estimate=pl.CostEstimate(
                flops=8 * pairs * lines * tokens * HD,
                bytes_accessed=8 * tokens * HD + 4 * pairs * lines * width,
                transcendentals=pairs * lines * tokens,
            ),
            name=body.__name__,
        )

    near_part = attend_lines(attend_sent, part_shape)(near, keys, values)
    with jax.named_scope("swap_parts"):
        far_part = partner(near_part)
    mean, logsum = attend_lines(attend_kept, (kept_shape, kept_shape))(far, keys, values)
    merged = pl.pallas_call(merge, out_shape=part_shape, compiler_params=small, name="merge")(
        mean, logsum, far_part
    )
    late_weight, merged = lax.optimization_barrier((out_weight, merged))
    other_weight = partner(late_weight)
    with jax.named_scope("scatter_rows"):
        parts = along_levels(merged)
    copies = pl.pallas_call(
        combine,
        out_shape=jax.ShapeDtypeStruct((pairs, own, heads * width), jnp.bfloat16),
        compiler_params=small,
        name="combine",
    )(parts)
    with jax.named_scope("gather_attended"):
        attended = along_levels(copies)
    in_vmem = pl.BlockSpec(memory_space=pltpu.VMEM)
    products = pl.pallas_call(
        project,
        in_specs=[pl.BlockSpec(memory_space=pltpu.SMEM), in_vmem, in_vmem, in_vmem],
        out_shape=jax.ShapeDtypeStruct((pairs, 2, own, out_weight.shape[1]), jnp.bfloat16),
        compiler_params=small,
        name="project",
    )(side.reshape(1), attended, out_weight, other_weight)
    with jax.named_scope("sum_heads"):
        shares = lax.all_to_all(
            products.reshape(2 * pairs, own, out_weight.shape[1]),
            ("head", "seq"),
            0,
            0,
            tiled=True,
            axis_index_groups=corners,
        )
        shares = shares.reshape(groups, 2 * own, out_weight.shape[1])
        return jnp.sum(shares.astype(jnp.float32), axis=0)


def solution(mesh):
    placed = (
        P(("rows", "seq"), "head", None),
        P(("rows", "seq")),
        P("seq", "head", None),
        P("seq", "head", None),
        P("seq", None, "head", None),
        P("seq", None, "head", None),
        P(),
        P(),
        P("head", "seq"),
    )
    return jax.shard_map(
        per_device,
        mesh=mesh,
        in_specs=placed,
        out_specs=P(("rows", "head"), "seq"),
        check_vma=False,
    )
```

```python
import functools
import math

import jax
import jax.numpy as jnp
from jax import lax
from jax.experimental import pallas as pl
from jax.experimental.pallas import tpu as pltpu
from jax.sharding import PartitionSpec as P

BLK = 128
ADAPTERS = 64
PATCHES = 4
HD = 128
RATE = math.log2(math.e) / math.sqrt(HD)
HIDDEN = -1e30
TAIL = 16
SPAN = 512
VMEM = 24 * 2**20


def pack(query_ref, adapter_ref, out_ref):
    rows, heads, width = query_ref.shape
    query = query_ref[...].astype(jnp.float32)
    line = lax.broadcasted_iota(jnp.int32, (rows, width), 0)
    lane = lax.broadcasted_iota(jnp.int32, (rows, width), 1)
    onehot = jnp.zeros((rows, width), jnp.float32)
    for r in range(rows):
        onehot = jnp.where((line == r) & (lane == adapter_ref[r]), 1.0, onehot)
    lines = [query[:, h, :] for h in range(heads)] + [onehot]
    message = jnp.concatenate(lines, 0).astype(jnp.bfloat16)
    for i in range(out_ref.shape[0]):
        out_ref[i] = message


def bar(slots, seq_ref, block_ref, slot_ref, *refs):
    out_ref = refs[-1]
    entries = block_ref.shape[1]
    blocks = out_ref.shape[0] // TAIL - slots
    line = lax.broadcasted_iota(jnp.int32, (blocks + slots, entries), 0)
    named = jnp.where(
        line < blocks,
        jnp.broadcast_to(block_ref[...], line.shape) - seq_ref[0] * blocks,
        jnp.broadcast_to(slot_ref[...], line.shape) - seq_ref[0] * slots + blocks,
    )
    entry = lax.broadcasted_iota(jnp.int32, (entries, HD), 0)
    adapter = lax.broadcasted_iota(jnp.int32, (entries, HD), 1)
    owns = jnp.where(entry // PATCHES == adapter, 1.0, 0.0).astype(jnp.bfloat16)
    hits = jnp.dot(
        jnp.where(named == line, 1.0, 0.0).astype(jnp.bfloat16),
        owns,
        preferred_element_type=jnp.float32,
    )
    is_block = lax.broadcasted_iota(jnp.int32, hits.shape, 0) < blocks
    hidden = jnp.where(is_block, hits, 1.0 - hits) > 0.5
    bars = jnp.where(hidden, HIDDEN, 0.0)
    for i in range(blocks + slots):
        out_ref[i * TAIL : (i + 1) * TAIL, :] = jnp.broadcast_to(
            bars[i : i + 1, :], (TAIL, HD)
        ).astype(jnp.bfloat16)


def store_part(out_ref, i, mean, logsum):
    lines = mean.shape[0]
    line = lax.broadcasted_iota(jnp.int32, (TAIL, lines), 0)
    out_ref[i, :lines, :] = mean.astype(jnp.bfloat16)
    flat = logsum
    first = flat.astype(jnp.bfloat16).astype(jnp.float32)
    second = (flat - first).astype(jnp.bfloat16).astype(jnp.float32)
    third = flat - first - second
    tail = jnp.where(
        line == 0, first, jnp.where(line == 1, second, jnp.where(line == 2, third, 0.0))
    )
    out_ref[i, lines:, :] = tail.astype(jnp.bfloat16)


def local_attention(msg_ref, doc_ref, patch_ref, doc_values_ref, patch_values_ref, bars_ref):
    count = msg_ref.shape[0]
    lines = msg_ref.shape[1] - TAIL
    heads = lines // TAIL
    parts = []
    for i in range(count):
        onehot = msg_ref[i, lines:, :]
        parts.append(
            jnp.concatenate(
                [msg_ref[i, :lines, :], jnp.concatenate([onehot] * heads, 0)], 1
            )
        )
    query = jnp.concatenate(parts, 0)
    ones = jnp.ones((SPAN, HD), jnp.bfloat16)
    peak = accum = None
    bar = 0
    for keys_ref, values_ref in ((doc_ref, doc_values_ref), (patch_ref, patch_values_ref)):
        for start in range(0, keys_ref.shape[0], SPAN):
            bars = []
            for _ in range(SPAN // BLK):
                bars += [bars_ref[bar * TAIL : (bar + 1) * TAIL, :]] * (BLK // TAIL)
                bar += 1
            keys = jnp.concatenate(
                [keys_ref[start : start + SPAN, :], jnp.concatenate(bars, 0)], 1
            )
            values = jnp.concatenate([values_ref[start : start + SPAN, :], ones], 1)
            scores = lax.dot_general(
                query, keys, (((1,), (1,)), ((), ())), preferred_element_type=jnp.float32
            )
            top = jnp.max(scores, axis=1, keepdims=True)
            if accum is not None:
                top = jnp.maximum(peak, top)
            weights = jnp.exp2((scores - top) * RATE).astype(jnp.bfloat16)
            added = jnp.dot(weights, values, preferred_element_type=jnp.float32)
            accum = added if accum is None else accum * jnp.exp2((peak - top) * RATE) + added
            peak = top
    total = accum[:, HD:]
    mean = accum[:, :HD] / total
    return mean, peak * RATE + jnp.log2(total)


def attend_sent(msg_ref, *refs):
    *local, out_ref = refs
    mean, logsum = local_attention(msg_ref, *local)
    lines = msg_ref.shape[1] - TAIL
    for i in range(msg_ref.shape[0]):
        store_part(
            out_ref,
            i,
            mean[i * lines : (i + 1) * lines],
            jnp.transpose(logsum[i * lines : (i + 1) * lines])[:TAIL, :],
        )


def attend_kept(msg_ref, *refs):
    *local, mean_ref, logsum_ref = refs
    mean, logsum = local_attention(msg_ref, *local)
    lines = msg_ref.shape[1] - TAIL
    for i in range(msg_ref.shape[0]):
        mean_ref[i] = mean[i * lines : (i + 1) * lines]
        logsum_ref[i : i + 1, :] = jnp.transpose(logsum[i * lines : (i + 1) * lines])[:1, :]


def columns(flat, lines):
    count = flat.shape[0]
    return jnp.transpose(
        jnp.concatenate([flat, jnp.zeros((lines - count, lines), jnp.float32)], 0)
    )


def merge(mean_ref, logsum_ref, two_ref, out_ref):
    count = two_ref.shape[0]
    lines = two_ref.shape[1] - TAIL
    one = logsum_ref[...]
    two = jnp.sum(two_ref[:, lines:, :].astype(jnp.float32), axis=1)
    top = jnp.maximum(one, two)
    first, second = jnp.exp2(one - top), jnp.exp2(two - top)
    both = first + second
    shares = columns(jnp.concatenate([first / both, second / both], 0), lines)
    logsum = top + jnp.log2(both)
    for i in range(count):
        mean = (
            mean_ref[i] * shares[:, i : i + 1]
            + two_ref[i, :lines, :].astype(jnp.float32) * shares[:, count + i : count + i + 1]
        )
        store_part(out_ref, i, mean, jnp.broadcast_to(logsum[i : i + 1, :], (TAIL, lines)))


def combine(parts_ref, out_ref):
    count = parts_ref.shape[0]
    lines = parts_ref.shape[1] - TAIL
    heads = lines // TAIL
    logsum = jnp.sum(parts_ref[:, lines:, :].astype(jnp.float32), axis=1)
    share = jnp.exp2(logsum - jnp.max(logsum, axis=0, keepdims=True))
    share = columns(share / jnp.sum(share, axis=0, keepdims=True), lines)
    mixed = None
    for i in range(count):
        term = parts_ref[i, :lines, :].astype(jnp.float32) * share[:, i : i + 1]
        mixed = term if mixed is None else mixed + term
    attended = mixed.astype(jnp.bfloat16)
    wide = jnp.concatenate([attended[h * TAIL : (h + 1) * TAIL] for h in range(heads)], 1)
    for i in range(out_ref.shape[0]):
        out_ref[i] = wide


def project(side_ref, rows_ref, own_ref, other_ref, out_ref):
    side = side_ref[0]
    count, own = rows_ref.shape[0], rows_ref.shape[1]
    rows = jnp.concatenate([rows_ref[i] for i in range(count)], 0)
    for weight_ref, place in ((own_ref, 1 - side), (other_ref, side)):
        product = jnp.dot(rows, weight_ref[...], preferred_element_type=jnp.float32)
        product = product.astype(jnp.bfloat16)
        for i in range(count):
            out_ref[i, place] = product[i * own : (i + 1) * own]


def per_device(
    queries,
    row_adapter,
    doc_keys,
    doc_values,
    patch_keys,
    patch_values,
    patch_block,
    patch_slot,
    out_weight,
):
    seqs = lax.axis_size("seq")
    groups = lax.axis_size("head")
    pairs = seqs // 2
    own, heads, width = queries.shape
    lines = own * heads
    seq_index = lax.axis_index("seq")
    side = lax.rem(seq_index, 2)
    adapter_ids = jnp.arange(HD, dtype=jnp.int32)
    levels = [[2 * level + at for level in range(pairs)] for at in range(2)]
    corners = [
        [head * seqs + 2 * level + at for head in range(groups) for at in (1, 0)]
        for level in range(pairs)
    ]

    def partner(array):
        return lax.ppermute(array, "seq", [(i, i ^ 1) for i in range(seqs)])

    def along_levels(array):
        return lax.all_to_all(array, "seq", 0, 0, tiled=True, axis_index_groups=levels)

    vmem = pltpu.CompilerParams(vmem_limit_bytes=VMEM)
    small = pltpu.CompilerParams(vmem_limit_bytes=16 * 2**20)
    part_shape = jax.ShapeDtypeStruct((pairs, lines + TAIL, width), jnp.bfloat16)

    message = pl.pallas_call(
        pack,
        in_specs=[
            pl.BlockSpec(memory_space=pltpu.VMEM),
            pl.BlockSpec(memory_space=pltpu.SMEM),
        ],
        out_shape=part_shape,
        compiler_params=pltpu.CompilerParams(vmem_limit_bytes=60 * 2**20),
        name="pack",
    )(queries, row_adapter)
    with jax.named_scope("gather_queries"):
        near = along_levels(message)
        far = partner(near)
    doc_len = doc_keys.shape[0]
    slots_here = patch_keys.shape[0]
    tokens = doc_len + slots_here * BLK
    in_vmem = pl.BlockSpec(memory_space=pltpu.VMEM)
    in_smem = pl.BlockSpec(memory_space=pltpu.SMEM)
    local = (
        doc_keys.reshape(doc_len, width),
        patch_keys.reshape(slots_here * BLK, width),
        doc_values.reshape(doc_len, width),
        patch_values.reshape(slots_here * BLK, width),
    )
    bars = pl.pallas_call(
        functools.partial(bar, slots_here),
        in_specs=[in_smem] + [in_vmem] * 6,
        out_shape=jax.ShapeDtypeStruct((tokens // BLK * TAIL, HD), jnp.bfloat16),
        compiler_params=small,
        name="bar",
    )(seq_index.reshape(1), patch_block.reshape(1, -1), patch_slot.reshape(1, -1), *local)
    local += (bars,)

    kept_shapes = (
        jax.ShapeDtypeStruct((pairs, lines, width), jnp.float32),
        jax.ShapeDtypeStruct((pairs, lines), jnp.float32),
    )

    def attend_lines(body, out_shape):
        return pl.pallas_call(
            body,
            out_shape=out_shape,
            compiler_params=vmem,
            cost_estimate=pl.CostEstimate(
                flops=8 * pairs * lines * tokens * HD,
                bytes_accessed=8 * tokens * HD + 4 * pairs * lines * width,
                transcendentals=pairs * lines * tokens,
            ),
            name=body.__name__,
        )

    near_part = attend_lines(attend_sent, part_shape)(near, *local)
    with jax.named_scope("swap_parts"):
        far_part = partner(near_part)
    mean, logsum = attend_lines(attend_kept, kept_shapes)(far, *local)
    merged = pl.pallas_call(merge, out_shape=part_shape, compiler_params=small, name="merge")(
        mean, logsum, far_part
    )
    late_weight, merged = lax.optimization_barrier((out_weight, merged))
    other_weight = partner(late_weight)
    with jax.named_scope("scatter_rows"):
        parts = along_levels(merged)
    copies = pl.pallas_call(
        combine,
        out_shape=jax.ShapeDtypeStruct((pairs, own, heads * width), jnp.bfloat16),
        compiler_params=small,
        name="combine",
    )(parts)
    with jax.named_scope("gather_attended"):
        attended = along_levels(copies)
    products = pl.pallas_call(
        project,
        in_specs=[in_smem] + [in_vmem] * 3,
        out_shape=jax.ShapeDtypeStruct((pairs, 2, own, out_weight.shape[1]), jnp.bfloat16),
        compiler_params=small,
        name="project",
    )(side.reshape(1), attended, out_weight, other_weight)
    with jax.named_scope("sum_heads"):
        shares = lax.all_to_all(
            products.reshape(2 * pairs, own, out_weight.shape[1]),
            ("head", "seq"),
            0,
            0,
            tiled=True,
            axis_index_groups=corners,
        )
        shares = shares.reshape(groups, 2 * own, out_weight.shape[1])
        return jnp.sum(shares.astype(jnp.float32), axis=0)


def solution(mesh):
    placed = (
        P(("rows", "seq"), "head", None),
        P(("rows", "seq")),
        P("seq", "head", None),
        P("seq", "head", None),
        P("seq", None, "head", None),
        P("seq", None, "head", None),
        P(),
        P(),
        P("head", "seq"),
    )
    return jax.shard_map(
        per_device,
        mesh=mesh,
        in_specs=placed,
        out_specs=P(("rows", "head"), "seq"),
        check_vma=False,
    )
```

```python
import functools
import math

import jax
import jax.numpy as jnp
from jax import lax
from jax.experimental import pallas as pl
from jax.experimental.pallas import tpu as pltpu
from jax.sharding import PartitionSpec as P

BLK = 128
ADAPTERS = 64
PATCHES = 4
HD = 128
RATE = math.log2(math.e) / math.sqrt(HD)
HIDDEN = -1e30
TAIL = 16
SPAN = 512
VMEM = 24 * 2**20


def pack(query_ref, adapter_ref, out_ref):
    rows, heads, width = query_ref.shape
    query = query_ref[...].astype(jnp.float32)
    line = lax.broadcasted_iota(jnp.int32, (rows, width), 0)
    lane = lax.broadcasted_iota(jnp.int32, (rows, width), 1)
    onehot = jnp.zeros((rows, width), jnp.float32)
    for r in range(rows):
        onehot = jnp.where((line == r) & (lane == adapter_ref[r]), 1.0, onehot)
    lines = [query[:, h, :] for h in range(heads)] + [onehot]
    message = jnp.concatenate(lines, 0).astype(jnp.bfloat16)
    for i in range(out_ref.shape[0]):
        out_ref[i] = message


def bar(slots, seq_ref, block_ref, slot_ref, *refs):
    first_ref, second_ref = refs[-2:]
    entries = block_ref.shape[1]
    blocks = first_ref.shape[0] // TAIL - slots
    line = lax.broadcasted_iota(jnp.int32, (blocks + slots, entries), 0)
    named = jnp.where(
        line < blocks,
        jnp.broadcast_to(block_ref[...], line.shape) - seq_ref[0] * blocks,
        jnp.broadcast_to(slot_ref[...], line.shape) - seq_ref[0] * slots + blocks,
    )
    entry = lax.broadcasted_iota(jnp.int32, (entries, HD), 0)
    adapter = lax.broadcasted_iota(jnp.int32, (entries, HD), 1)
    owns = jnp.where(entry // PATCHES == adapter, 1.0, 0.0).astype(jnp.bfloat16)
    hits = jnp.dot(
        jnp.where(named == line, 1.0, 0.0).astype(jnp.bfloat16),
        owns,
        preferred_element_type=jnp.float32,
    )
    is_block = lax.broadcasted_iota(jnp.int32, hits.shape, 0) < blocks
    hidden = jnp.where(is_block, hits, 1.0 - hits) > 0.5
    bars = jnp.where(hidden, HIDDEN, 0.0)
    for i in range(blocks + slots):
        tile = jnp.broadcast_to(bars[i : i + 1, :], (TAIL, HD)).astype(jnp.bfloat16)
        first_ref[i * TAIL : (i + 1) * TAIL, :] = tile
        second_ref[i * TAIL : (i + 1) * TAIL, :] = tile


def store_part(out_ref, i, mean, logsum):
    lines = mean.shape[0]
    line = lax.broadcasted_iota(jnp.int32, (TAIL, lines), 0)
    out_ref[i, :lines, :] = mean.astype(jnp.bfloat16)
    flat = logsum
    first = flat.astype(jnp.bfloat16).astype(jnp.float32)
    second = (flat - first).astype(jnp.bfloat16).astype(jnp.float32)
    third = flat - first - second
    tail = jnp.where(
        line == 0, first, jnp.where(line == 1, second, jnp.where(line == 2, third, 0.0))
    )
    out_ref[i, lines:, :] = tail.astype(jnp.bfloat16)


def local_attention(msg_ref, doc_ref, patch_ref, doc_values_ref, patch_values_ref, bars_ref):
    count = msg_ref.shape[0]
    lines = msg_ref.shape[1] - TAIL
    heads = lines // TAIL
    parts = []
    for i in range(count):
        onehot = msg_ref[i, lines:, :]
        parts.append(
            jnp.concatenate(
                [msg_ref[i, :lines, :], jnp.concatenate([onehot] * heads, 0)], 1
            )
        )
    query = jnp.concatenate(parts, 0)
    ones = jnp.ones((SPAN, HD), jnp.bfloat16)
    peak = accum = None
    bar = 0
    for keys_ref, values_ref in ((doc_ref, doc_values_ref), (patch_ref, patch_values_ref)):
        for start in range(0, keys_ref.shape[0], SPAN):
            bars = []
            for _ in range(SPAN // BLK):
                bars += [bars_ref[bar * TAIL : (bar + 1) * TAIL, :]] * (BLK // TAIL)
                bar += 1
            keys = jnp.concatenate(
                [keys_ref[start : start + SPAN, :], jnp.concatenate(bars, 0)], 1
            )
            values = jnp.concatenate([values_ref[start : start + SPAN, :], ones], 1)
            scores = lax.dot_general(
                query, keys, (((1,), (1,)), ((), ())), preferred_element_type=jnp.float32
            )
            top = jnp.max(scores, axis=1, keepdims=True)
            if accum is not None:
                top = jnp.maximum(peak, top)
            weights = jnp.exp2((scores - top) * RATE).astype(jnp.bfloat16)
            added = jnp.dot(weights, values, preferred_element_type=jnp.float32)
            accum = added if accum is None else accum * jnp.exp2((peak - top) * RATE) + added
            peak = top
    total = accum[:, HD:]
    mean = accum[:, :HD] / total
    return mean, peak * RATE + jnp.log2(total)


def attend_sent(msg_ref, *refs):
    *local, out_ref = refs
    mean, logsum = local_attention(msg_ref, *local)
    lines = msg_ref.shape[1] - TAIL
    for i in range(msg_ref.shape[0]):
        store_part(
            out_ref,
            i,
            mean[i * lines : (i + 1) * lines],
            jnp.transpose(logsum[i * lines : (i + 1) * lines])[:TAIL, :],
        )


def attend_kept(msg_ref, *refs):
    *local, mean_ref, logsum_ref = refs
    mean, logsum = local_attention(msg_ref, *local)
    lines = msg_ref.shape[1] - TAIL
    for i in range(msg_ref.shape[0]):
        mean_ref[i] = mean[i * lines : (i + 1) * lines]
        logsum_ref[i : i + 1, :] = jnp.transpose(logsum[i * lines : (i + 1) * lines])[:1, :]


def columns(flat, lines):
    count = flat.shape[0]
    return jnp.transpose(
        jnp.concatenate([flat, jnp.zeros((lines - count, lines), jnp.float32)], 0)
    )


def merge(mean_ref, logsum_ref, two_ref, out_ref):
    count = two_ref.shape[0]
    lines = two_ref.shape[1] - TAIL
    one = logsum_ref[...]
    two = jnp.sum(two_ref[:, lines:, :].astype(jnp.float32), axis=1)
    top = jnp.maximum(one, two)
    first, second = jnp.exp2(one - top), jnp.exp2(two - top)
    both = first + second
    shares = columns(jnp.concatenate([first / both, second / both], 0), lines)
    logsum = top + jnp.log2(both)
    for i in range(count):
        mean = (
            mean_ref[i] * shares[:, i : i + 1]
            + two_ref[i, :lines, :].astype(jnp.float32) * shares[:, count + i : count + i + 1]
        )
        store_part(out_ref, i, mean, jnp.broadcast_to(logsum[i : i + 1, :], (TAIL, lines)))


def combine(parts_ref, out_ref):
    count = parts_ref.shape[0]
    lines = parts_ref.shape[1] - TAIL
    heads = lines // TAIL
    logsum = jnp.sum(parts_ref[:, lines:, :].astype(jnp.float32), axis=1)
    share = jnp.exp2(logsum - jnp.max(logsum, axis=0, keepdims=True))
    share = columns(share / jnp.sum(share, axis=0, keepdims=True), lines)
    mixed = None
    for i in range(count):
        term = parts_ref[i, :lines, :].astype(jnp.float32) * share[:, i : i + 1]
        mixed = term if mixed is None else mixed + term
    attended = mixed.astype(jnp.bfloat16)
    wide = jnp.concatenate([attended[h * TAIL : (h + 1) * TAIL] for h in range(heads)], 1)
    for i in range(out_ref.shape[0]):
        out_ref[i] = wide


def project(side_ref, rows_ref, own_ref, other_ref, out_ref):
    side = side_ref[0]
    count, own = rows_ref.shape[0], rows_ref.shape[1]
    rows = jnp.concatenate([rows_ref[i] for i in range(count)], 0)
    for weight_ref, place in ((own_ref, 1 - side), (other_ref, side)):
        product = jnp.dot(rows, weight_ref[...], preferred_element_type=jnp.float32)
        product = product.astype(jnp.bfloat16)
        for i in range(count):
            out_ref[i, place] = product[i * own : (i + 1) * own]


def per_device(
    queries,
    row_adapter,
    doc_keys,
    doc_values,
    patch_keys,
    patch_values,
    patch_block,
    patch_slot,
    out_weight,
):
    seqs = lax.axis_size("seq")
    groups = lax.axis_size("head")
    pairs = seqs // 2
    own, heads, width = queries.shape
    lines = own * heads
    seq_index = lax.axis_index("seq")
    side = lax.rem(seq_index, 2)
    adapter_ids = jnp.arange(HD, dtype=jnp.int32)
    levels = [[2 * level + at for level in range(pairs)] for at in range(2)]
    corners = [
        [head * seqs + 2 * level + at for head in range(groups) for at in (1, 0)]
        for level in range(pairs)
    ]

    def partner(array):
        return lax.ppermute(array, "seq", [(i, i ^ 1) for i in range(seqs)])

    def along_levels(array):
        return lax.all_to_all(array, "seq", 0, 0, tiled=True, axis_index_groups=levels)

    vmem = pltpu.CompilerParams(vmem_limit_bytes=VMEM)
    small = pltpu.CompilerParams(vmem_limit_bytes=16 * 2**20)

    def cost(flops, size):
        return pl.CostEstimate(flops=flops, bytes_accessed=size, transcendentals=0)

    part_shape = jax.ShapeDtypeStruct((pairs, lines + TAIL, width), jnp.bfloat16)

    message = pl.pallas_call(
        pack,
        in_specs=[
            pl.BlockSpec(memory_space=pltpu.VMEM),
            pl.BlockSpec(memory_space=pltpu.SMEM),
        ],
        out_shape=part_shape,
        compiler_params=pltpu.CompilerParams(vmem_limit_bytes=60 * 2**20),
        name="pack",
    )(queries, row_adapter)
    with jax.named_scope("gather_queries"):
        near = along_levels(message)
        far = partner(near)
    doc_len = doc_keys.shape[0]
    slots_here = patch_keys.shape[0]
    tokens = doc_len + slots_here * BLK
    in_vmem = pl.BlockSpec(memory_space=pltpu.VMEM)
    in_smem = pl.BlockSpec(memory_space=pltpu.SMEM)
    local = (
        doc_keys.reshape(doc_len, width),
        patch_keys.reshape(slots_here * BLK, width),
        doc_values.reshape(doc_len, width),
        patch_values.reshape(slots_here * BLK, width),
    )
    first_bars, second_bars = pl.pallas_call(
        functools.partial(bar, slots_here),
        in_specs=[in_smem] + [in_vmem] * 6,
        out_shape=[jax.ShapeDtypeStruct((tokens // BLK * TAIL, HD), jnp.bfloat16)] * 2,
        compiler_params=small,
        cost_estimate=cost(10**7, 10**6),
        name="bar",
    )(seq_index.reshape(1), patch_block.reshape(1, -1), patch_slot.reshape(1, -1), *local)

    kept_shapes = (
        jax.ShapeDtypeStruct((pairs, lines, width), jnp.float32),
        jax.ShapeDtypeStruct((pairs, lines), jnp.float32),
    )

    def attend_lines(body, out_shape):
        return pl.pallas_call(
            body,
            out_shape=out_shape,
            compiler_params=vmem,
            cost_estimate=pl.CostEstimate(
                flops=8 * pairs * lines * tokens * HD,
                bytes_accessed=8 * tokens * HD + 4 * pairs * lines * width,
                transcendentals=pairs * lines * tokens,
            ),
            name=body.__name__,
        )

    near_part = attend_lines(attend_sent, part_shape)(near, *local, first_bars)
    with jax.named_scope("swap_parts"):
        far_part = partner(near_part)
    mean, logsum = attend_lines(attend_kept, kept_shapes)(far, *local, second_bars)
    merged = pl.pallas_call(
        merge,
        out_shape=part_shape,
        compiler_params=small,
        cost_estimate=cost(10**6, 10**6),
        name="merge",
    )(mean, logsum, far_part)
    late_weight, merged = lax.optimization_barrier((out_weight, merged))
    other_weight = partner(late_weight)
    with jax.named_scope("scatter_rows"):
        parts = along_levels(merged)
    copies = pl.pallas_call(
        combine,
        out_shape=jax.ShapeDtypeStruct((pairs, own, heads * width), jnp.bfloat16),
        compiler_params=small,
        cost_estimate=cost(10**6, 10**6),
        name="combine",
    )(parts)
    with jax.named_scope("gather_attended"):
        attended = along_levels(copies)
    products = pl.pallas_call(
        project,
        in_specs=[in_smem] + [in_vmem] * 3,
        out_shape=jax.ShapeDtypeStruct((pairs, 2, own, out_weight.shape[1]), jnp.bfloat16),
        compiler_params=small,
        cost_estimate=cost(3 * 10**8, 2 * 10**6),
        name="project",
    )(side.reshape(1), attended, out_weight, other_weight)
    with jax.named_scope("sum_heads"):
        shares = lax.all_to_all(
            products.reshape(2 * pairs, own, out_weight.shape[1]),
            ("head", "seq"),
            0,
            0,
            tiled=True,
            axis_index_groups=corners,
        )
        shares = shares.reshape(groups, 2 * own, out_weight.shape[1])
        return jnp.sum(shares.astype(jnp.float32), axis=0)


def solution(mesh):
    placed = (
        P(("rows", "seq"), "head", None),
        P(("rows", "seq")),
        P("seq", "head", None),
        P("seq", "head", None),
        P("seq", None, "head", None),
        P("seq", None, "head", None),
        P(),
        P(),
        P("head", "seq"),
    )
    return jax.shard_map(
        per_device,
        mesh=mesh,
        in_specs=placed,
        out_specs=P(("rows", "head"), "seq"),
        check_vma=False,
    )
```

```python
import functools
import math

import jax
import jax.numpy as jnp
from jax import lax
from jax.experimental import pallas as pl
from jax.experimental.pallas import tpu as pltpu
from jax.sharding import PartitionSpec as P

BLK = 128
ADAPTERS = 64
PATCHES = 4
HD = 128
RATE = math.log2(math.e) / math.sqrt(HD)
HIDDEN = -1e30
TAIL = 16
SPAN = 512
VMEM = 24 * 2**20


def pack(query_ref, adapter_ref, out_ref):
    rows, heads, width = query_ref.shape
    query = query_ref[...].astype(jnp.float32)
    line = lax.broadcasted_iota(jnp.int32, (rows, width), 0)
    lane = lax.broadcasted_iota(jnp.int32, (rows, width), 1)
    onehot = jnp.zeros((rows, width), jnp.float32)
    for r in range(rows):
        onehot = jnp.where((line == r) & (lane == adapter_ref[r]), 1.0, onehot)
    lines = [query[:, h, :] for h in range(heads)] + [onehot]
    message = jnp.concatenate(lines, 0).astype(jnp.bfloat16)
    for i in range(out_ref.shape[0]):
        out_ref[i] = message


def bar(slots, seq_ref, block_ref, slot_ref, *refs):
    first_ref, second_ref = refs[-2:]
    entries = block_ref.shape[1]
    blocks = first_ref.shape[0] - slots
    line = lax.broadcasted_iota(jnp.int32, (blocks + slots, entries), 0)
    named = jnp.where(
        line < blocks,
        jnp.broadcast_to(block_ref[...], line.shape) - seq_ref[0] * blocks,
        jnp.broadcast_to(slot_ref[...], line.shape) - seq_ref[0] * slots + blocks,
    )
    entry = lax.broadcasted_iota(jnp.int32, (entries, HD), 0)
    adapter = lax.broadcasted_iota(jnp.int32, (entries, HD), 1)
    owns = jnp.where(entry // PATCHES == adapter, 1.0, 0.0).astype(jnp.bfloat16)
    hits = jnp.dot(
        jnp.where(named == line, 1.0, 0.0).astype(jnp.bfloat16),
        owns,
        preferred_element_type=jnp.float32,
    )
    is_block = lax.broadcasted_iota(jnp.int32, hits.shape, 0) < blocks
    hidden = jnp.where(is_block, hits, 1.0 - hits) > 0.5
    bars = jnp.where(hidden, HIDDEN, 0.0)
    first_ref[...] = bars
    second_ref[...] = bars


def store_part(out_ref, i, mean, logsum):
    lines = mean.shape[0]
    line = lax.broadcasted_iota(jnp.int32, (TAIL, lines), 0)
    out_ref[i, :lines, :] = mean.astype(jnp.bfloat16)
    flat = logsum
    first = flat.astype(jnp.bfloat16).astype(jnp.float32)
    second = (flat - first).astype(jnp.bfloat16).astype(jnp.float32)
    third = flat - first - second
    tail = jnp.where(
        line == 0, first, jnp.where(line == 1, second, jnp.where(line == 2, third, 0.0))
    )
    out_ref[i, lines:, :] = tail.astype(jnp.bfloat16)


def local_attention(msg_ref, doc_ref, doc_values_ref, patches_ref, bars_ref):
    count = msg_ref.shape[0]
    lines = msg_ref.shape[1] - TAIL
    heads = lines // TAIL
    parts = []
    for i in range(count):
        onehot = msg_ref[i, lines:, :]
        parts.append(
            jnp.concatenate(
                [msg_ref[i, :lines, :], jnp.concatenate([onehot] * heads, 0)], 1
            )
        )
    query = jnp.concatenate(parts, 0)
    ones = jnp.ones((SPAN, HD), jnp.bfloat16)
    peak = accum = None
    bar = 0
    patch_len = patches_ref.shape[0] // 2
    patch_ref = patches_ref.at[pl.ds(0, patch_len)]
    patch_values_ref = patches_ref.at[pl.ds(patch_len, patch_len)]
    for keys_ref, values_ref in ((doc_ref, doc_values_ref), (patch_ref, patch_values_ref)):
        for start in range(0, keys_ref.shape[0], SPAN):
            bars = []
            for _ in range(SPAN // BLK):
                tile = jnp.broadcast_to(bars_ref[bar : bar + 1, :], (TAIL, HD))
                bars += [tile.astype(jnp.bfloat16)] * (BLK // TAIL)
                bar += 1
            keys = jnp.concatenate(
                [keys_ref[start : start + SPAN, :], jnp.concatenate(bars, 0)], 1
            )
            values = jnp.concatenate([values_ref[start : start + SPAN, :], ones], 1)
            scores = lax.dot_general(
                query, keys, (((1,), (1,)), ((), ())), preferred_element_type=jnp.float32
            )
            top = jnp.max(scores, axis=1, keepdims=True)
            if accum is not None:
                top = jnp.maximum(peak, top)
            weights = jnp.exp2((scores - top) * RATE).astype(jnp.bfloat16)
            added = jnp.dot(weights, values, preferred_element_type=jnp.float32)
            accum = added if accum is None else accum * jnp.exp2((peak - top) * RATE) + added
            peak = top
    total = accum[:, HD:]
    mean = accum[:, :HD] / total
    return mean, peak * RATE + jnp.log2(total)


def attend_sent(msg_ref, *refs):
    *local, out_ref = refs
    mean, logsum = local_attention(msg_ref, *local)
    lines = msg_ref.shape[1] - TAIL
    for i in range(msg_ref.shape[0]):
        store_part(
            out_ref,
            i,
            mean[i * lines : (i + 1) * lines],
            jnp.transpose(logsum[i * lines : (i + 1) * lines])[:TAIL, :],
        )


def attend_kept(msg_ref, *refs):
    *local, mean_ref, logsum_ref = refs
    mean, logsum = local_attention(msg_ref, *local)
    lines = msg_ref.shape[1] - TAIL
    for i in range(msg_ref.shape[0]):
        mean_ref[i] = mean[i * lines : (i + 1) * lines]
        logsum_ref[i : i + 1, :] = jnp.transpose(logsum[i * lines : (i + 1) * lines])[:1, :]


def columns(flat, lines):
    count = flat.shape[0]
    return jnp.transpose(
        jnp.concatenate([flat, jnp.zeros((lines - count, lines), jnp.float32)], 0)
    )


def merge(mean_ref, logsum_ref, two_ref, out_ref):
    count = two_ref.shape[0]
    lines = two_ref.shape[1] - TAIL
    one = logsum_ref[...]
    two = jnp.sum(two_ref[:, lines:, :].astype(jnp.float32), axis=1)
    top = jnp.maximum(one, two)
    first, second = jnp.exp2(one - top), jnp.exp2(two - top)
    both = first + second
    shares = columns(jnp.concatenate([first / both, second / both], 0), lines)
    logsum = top + jnp.log2(both)
    for i in range(count):
        mean = (
            mean_ref[i] * shares[:, i : i + 1]
            + two_ref[i, :lines, :].astype(jnp.float32) * shares[:, count + i : count + i + 1]
        )
        store_part(out_ref, i, mean, jnp.broadcast_to(logsum[i : i + 1, :], (TAIL, lines)))


def combine(parts_ref, out_ref):
    count = parts_ref.shape[0]
    lines = parts_ref.shape[1] - TAIL
    heads = lines // TAIL
    logsum = jnp.sum(parts_ref[:, lines:, :].astype(jnp.float32), axis=1)
    share = jnp.exp2(logsum - jnp.max(logsum, axis=0, keepdims=True))
    share = columns(share / jnp.sum(share, axis=0, keepdims=True), lines)
    mixed = None
    for i in range(count):
        term = parts_ref[i, :lines, :].astype(jnp.float32) * share[:, i : i + 1]
        mixed = term if mixed is None else mixed + term
    attended = mixed.astype(jnp.bfloat16)
    wide = jnp.concatenate([attended[h * TAIL : (h + 1) * TAIL] for h in range(heads)], 1)
    for i in range(out_ref.shape[0]):
        out_ref[i] = wide


def project(side_ref, rows_ref, own_ref, other_ref, out_ref):
    side = side_ref[0]
    count, own = rows_ref.shape[0], rows_ref.shape[1]
    rows = jnp.concatenate([rows_ref[i] for i in range(count)], 0)
    for weight_ref, place in ((own_ref, 1 - side), (other_ref, side)):
        product = jnp.dot(rows, weight_ref[...], preferred_element_type=jnp.float32)
        product = product.astype(jnp.bfloat16)
        for i in range(count):
            out_ref[i, place] = product[i * own : (i + 1) * own]


def per_device(
    queries,
    row_adapter,
    doc_keys,
    doc_values,
    patch_keys,
    patch_values,
    patch_block,
    patch_slot,
    out_weight,
):
    seqs = lax.axis_size("seq")
    groups = lax.axis_size("head")
    pairs = seqs // 2
    own, heads, width = queries.shape
    lines = own * heads
    seq_index = lax.axis_index("seq")
    side = lax.rem(seq_index, 2)
    adapter_ids = jnp.arange(HD, dtype=jnp.int32)
    levels = [[2 * level + at for level in range(pairs)] for at in range(2)]
    corners = [
        [head * seqs + 2 * level + at for head in range(groups) for at in (1, 0)]
        for level in range(pairs)
    ]

    def partner(array):
        return lax.ppermute(array, "seq", [(i, i ^ 1) for i in range(seqs)])

    def along_levels(array):
        return lax.all_to_all(array, "seq", 0, 0, tiled=True, axis_index_groups=levels)

    vmem = pltpu.CompilerParams(vmem_limit_bytes=VMEM)
    small = pltpu.CompilerParams(vmem_limit_bytes=16 * 2**20)

    def cost(flops, size):
        return pl.CostEstimate(flops=flops, bytes_accessed=size, transcendentals=0)

    part_shape = jax.ShapeDtypeStruct((pairs, lines + TAIL, width), jnp.bfloat16)

    message = pl.pallas_call(
        pack,
        in_specs=[
            pl.BlockSpec(memory_space=pltpu.VMEM),
            pl.BlockSpec(memory_space=pltpu.SMEM),
        ],
        out_shape=part_shape,
        compiler_params=pltpu.CompilerParams(vmem_limit_bytes=60 * 2**20),
        name="pack",
    )(queries, row_adapter)
    with jax.named_scope("gather_queries"):
        near = along_levels(message)
        far = partner(near)
    doc_len = doc_keys.shape[0]
    slots_here = patch_keys.shape[0]
    tokens = doc_len + slots_here * BLK
    in_vmem = pl.BlockSpec(memory_space=pltpu.VMEM)
    in_smem = pl.BlockSpec(memory_space=pltpu.SMEM)
    local = (
        doc_keys.reshape(doc_len, width),
        doc_values.reshape(doc_len, width),
        jnp.concatenate(
            [
                patch_keys.reshape(slots_here * BLK, width),
                patch_values.reshape(slots_here * BLK, width),
            ],
            0,
        ),
    )
    first_bars, second_bars = pl.pallas_call(
        functools.partial(bar, slots_here),
        in_specs=[in_smem] + [in_vmem] * 5,
        out_shape=[jax.ShapeDtypeStruct((tokens // BLK, HD), jnp.float32)] * 2,
        compiler_params=small,
        cost_estimate=cost(10**7, 10**6),
        name="bar",
    )(seq_index.reshape(1), patch_block.reshape(1, -1), patch_slot.reshape(1, -1), *local)

    kept_shapes = (
        jax.ShapeDtypeStruct((pairs, lines, width), jnp.float32),
        jax.ShapeDtypeStruct((pairs, lines), jnp.float32),
    )

    def attend_lines(body, out_shape):
        return pl.pallas_call(
            body,
            out_shape=out_shape,
            compiler_params=vmem,
            cost_estimate=pl.CostEstimate(
                flops=8 * pairs * lines * tokens * HD,
                bytes_accessed=8 * tokens * HD + 4 * pairs * lines * width,
                transcendentals=pairs * lines * tokens,
            ),
            name=body.__name__,
        )

    near_part = attend_lines(attend_sent, part_shape)(near, *local, first_bars)
    with jax.named_scope("swap_parts"):
        far_part = partner(near_part)
    mean, logsum = attend_lines(attend_kept, kept_shapes)(far, *local, second_bars)
    merged = pl.pallas_call(
        merge,
        out_shape=part_shape,
        compiler_params=small,
        cost_estimate=cost(10**6, 10**6),
        name="merge",
    )(mean, logsum, far_part)
    late_weight, merged = lax.optimization_barrier((out_weight, merged))
    other_weight = partner(late_weight)
    with jax.named_scope("scatter_rows"):
        parts = along_levels(merged)
    copies = pl.pallas_call(
        combine,
        out_shape=jax.ShapeDtypeStruct((pairs, own, heads * width), jnp.bfloat16),
        compiler_params=small,
        cost_estimate=cost(10**6, 10**6),
        name="combine",
    )(parts)
    with jax.named_scope("gather_attended"):
        attended = along_levels(copies)
    products = pl.pallas_call(
        project,
        in_specs=[in_smem] + [in_vmem] * 3,
        out_shape=jax.ShapeDtypeStruct((pairs, 2, own, out_weight.shape[1]), jnp.bfloat16),
        compiler_params=small,
        cost_estimate=cost(3 * 10**8, 2 * 10**6),
        name="project",
    )(side.reshape(1), attended, out_weight, other_weight)
    with jax.named_scope("sum_heads"):
        shares = lax.all_to_all(
            products.reshape(2 * pairs, own, out_weight.shape[1]),
            ("head", "seq"),
            0,
            0,
            tiled=True,
            axis_index_groups=corners,
        )
        shares = shares.reshape(groups, 2 * own, out_weight.shape[1])
        return jnp.sum(shares.astype(jnp.float32), axis=0)


def solution(mesh):
    placed = (
        P(("rows", "seq"), "head", None),
        P(("rows", "seq")),
        P("seq", "head", None),
        P("seq", "head", None),
        P("seq", None, "head", None),
        P("seq", None, "head", None),
        P(),
        P(),
        P("head", "seq"),
    )
    return jax.shard_map(
        per_device,
        mesh=mesh,
        in_specs=placed,
        out_specs=P(("rows", "head"), "seq"),
        check_vma=False,
    )
```

```python
import functools
import math

import jax
import jax.numpy as jnp
from jax import lax
from jax.experimental import pallas as pl
from jax.experimental.pallas import tpu as pltpu
from jax.sharding import PartitionSpec as P

BLK = 128
ADAPTERS = 64
PATCHES = 4
HD = 128
RATE = math.log2(math.e) / math.sqrt(HD)
HIDDEN = -1e30
TAIL = 16
SPAN = 512
OWN_SPAN = 2048
VMEM = 24 * 2**20


def pack(query_ref, adapter_ref, out_ref, own_ref):
    rows, heads, width = query_ref.shape
    query = query_ref[...].astype(jnp.float32)
    line = lax.broadcasted_iota(jnp.int32, (rows, width), 0)
    lane = lax.broadcasted_iota(jnp.int32, (rows, width), 1)
    onehot = jnp.zeros((rows, width), jnp.float32)
    for r in range(rows):
        onehot = jnp.where((line == r) & (lane == adapter_ref[r]), 1.0, onehot)
    lines = [query[:, h, :] for h in range(heads)] + [onehot]
    message = jnp.concatenate(lines, 0).astype(jnp.bfloat16)
    for i in range(out_ref.shape[0]):
        out_ref[i] = message
    own_ref[0] = message


def bar(slots, seq_ref, block_ref, slot_ref, *refs):
    bars_refs = refs[-3:]
    entries = block_ref.shape[1]
    blocks = bars_refs[0].shape[0] - slots
    line = lax.broadcasted_iota(jnp.int32, (blocks + slots, entries), 0)
    named = jnp.where(
        line < blocks,
        jnp.broadcast_to(block_ref[...], line.shape) - seq_ref[0] * blocks,
        jnp.broadcast_to(slot_ref[...], line.shape) - seq_ref[0] * slots + blocks,
    )
    entry = lax.broadcasted_iota(jnp.int32, (entries, HD), 0)
    adapter = lax.broadcasted_iota(jnp.int32, (entries, HD), 1)
    owns = jnp.where(entry // PATCHES == adapter, 1.0, 0.0).astype(jnp.bfloat16)
    hits = jnp.dot(
        jnp.where(named == line, 1.0, 0.0).astype(jnp.bfloat16),
        owns,
        preferred_element_type=jnp.float32,
    )
    is_block = lax.broadcasted_iota(jnp.int32, hits.shape, 0) < blocks
    hidden = jnp.where(is_block, hits, 1.0 - hits) > 0.5
    bars = jnp.where(hidden, HIDDEN, 0.0)
    for bars_ref in bars_refs:
        bars_ref[...] = bars


def store_part(out_ref, i, mean, logsum):
    lines = mean.shape[0]
    line = lax.broadcasted_iota(jnp.int32, (TAIL, lines), 0)
    out_ref[i, :lines, :] = mean.astype(jnp.bfloat16)
    flat = logsum
    first = flat.astype(jnp.bfloat16).astype(jnp.float32)
    second = (flat - first).astype(jnp.bfloat16).astype(jnp.float32)
    third = flat - first - second
    tail = jnp.where(
        line == 0, first, jnp.where(line == 1, second, jnp.where(line == 2, third, 0.0))
    )
    out_ref[i, lines:, :] = tail.astype(jnp.bfloat16)


def local_attention(places, span, msg_ref, doc_ref, doc_values_ref, patches_ref, bars_ref):
    lines = msg_ref.shape[1] - TAIL
    heads = lines // TAIL
    parts = []
    for i in places:
        onehot = msg_ref[i, lines:, :]
        parts.append(
            jnp.concatenate(
                [msg_ref[i, :lines, :], jnp.concatenate([onehot] * heads, 0)], 1
            )
        )
    query = jnp.concatenate(parts, 0)
    ones = jnp.ones((span, HD), jnp.bfloat16)
    peak = accum = None
    bar = 0
    patch_len = patches_ref.shape[0] // 2
    patch_ref = patches_ref.at[pl.ds(0, patch_len)]
    patch_values_ref = patches_ref.at[pl.ds(patch_len, patch_len)]
    for keys_ref, values_ref in ((doc_ref, doc_values_ref), (patch_ref, patch_values_ref)):
        for start in range(0, keys_ref.shape[0], span):
            bars = []
            for _ in range(span // BLK):
                tile = jnp.broadcast_to(bars_ref[bar : bar + 1, :], (TAIL, HD))
                bars += [tile.astype(jnp.bfloat16)] * (BLK // TAIL)
                bar += 1
            keys = jnp.concatenate(
                [keys_ref[start : start + span, :], jnp.concatenate(bars, 0)], 1
            )
            values = jnp.concatenate([values_ref[start : start + span, :], ones], 1)
            scores = lax.dot_general(
                query, keys, (((1,), (1,)), ((), ())), preferred_element_type=jnp.float32
            )
            top = jnp.max(scores, axis=1, keepdims=True)
            if accum is not None:
                top = jnp.maximum(peak, top)
            weights = jnp.exp2((scores - top) * RATE).astype(jnp.bfloat16)
            added = jnp.dot(weights, values, preferred_element_type=jnp.float32)
            accum = added if accum is None else accum * jnp.exp2((peak - top) * RATE) + added
            peak = top
    total = accum[:, HD:]
    mean = accum[:, :HD] / total
    return mean, peak * RATE + jnp.log2(total)


def attend_own(msg_ref, *refs):
    *local, out_ref = refs
    send(range(msg_ref.shape[0]), OWN_SPAN, msg_ref, local, out_ref)


def attend_rest(level_ref, own_ref, msg_ref, *refs):
    *local, out_ref = refs
    count = msg_ref.shape[0]
    out_ref[level_ref[0]] = own_ref[0]
    places = [lax.rem(level_ref[0] + i, count) for i in range(1, count)]
    send(places, SPAN, msg_ref, local, out_ref)


def send(places, span, msg_ref, local, out_ref):
    mean, logsum = local_attention(places, span, msg_ref, *local)
    lines = msg_ref.shape[1] - TAIL
    for i, place in enumerate(places):
        store_part(
            out_ref,
            place,
            mean[i * lines : (i + 1) * lines],
            jnp.transpose(logsum[i * lines : (i + 1) * lines])[:TAIL, :],
        )


def attend_kept(msg_ref, *refs):
    *local, mean_ref, logsum_ref = refs
    mean, logsum = local_attention(range(msg_ref.shape[0]), SPAN, msg_ref, *local)
    lines = msg_ref.shape[1] - TAIL
    for i in range(msg_ref.shape[0]):
        mean_ref[i] = mean[i * lines : (i + 1) * lines]
        logsum_ref[i : i + 1, :] = jnp.transpose(logsum[i * lines : (i + 1) * lines])[:1, :]


def columns(flat, lines):
    count = flat.shape[0]
    return jnp.transpose(
        jnp.concatenate([flat, jnp.zeros((lines - count, lines), jnp.float32)], 0)
    )


def merge(mean_ref, logsum_ref, two_ref, out_ref):
    count = two_ref.shape[0]
    lines = two_ref.shape[1] - TAIL
    one = logsum_ref[...]
    two = jnp.sum(two_ref[:, lines:, :].astype(jnp.float32), axis=1)
    top = jnp.maximum(one, two)
    first, second = jnp.exp2(one - top), jnp.exp2(two - top)
    both = first + second
    shares = columns(jnp.concatenate([first / both, second / both], 0), lines)
    logsum = top + jnp.log2(both)
    for i in range(count):
        mean = (
            mean_ref[i] * shares[:, i : i + 1]
            + two_ref[i, :lines, :].astype(jnp.float32) * shares[:, count + i : count + i + 1]
        )
        store_part(out_ref, i, mean, jnp.broadcast_to(logsum[i : i + 1, :], (TAIL, lines)))


def combine(parts_ref, out_ref):
    count = parts_ref.shape[0]
    lines = parts_ref.shape[1] - TAIL
    heads = lines // TAIL
    logsum = jnp.sum(parts_ref[:, lines:, :].astype(jnp.float32), axis=1)
    share = jnp.exp2(logsum - jnp.max(logsum, axis=0, keepdims=True))
    share = columns(share / jnp.sum(share, axis=0, keepdims=True), lines)
    mixed = None
    for i in range(count):
        term = parts_ref[i, :lines, :].astype(jnp.float32) * share[:, i : i + 1]
        mixed = term if mixed is None else mixed + term
    attended = mixed.astype(jnp.bfloat16)
    wide = jnp.concatenate([attended[h * TAIL : (h + 1) * TAIL] for h in range(heads)], 1)
    for i in range(out_ref.shape[0]):
        out_ref[i] = wide


def project(side_ref, rows_ref, own_ref, other_ref, out_ref):
    side = side_ref[0]
    count, own = rows_ref.shape[0], rows_ref.shape[1]
    rows = jnp.concatenate([rows_ref[i] for i in range(count)], 0)
    for weight_ref, place in ((own_ref, 1 - side), (other_ref, side)):
        product = jnp.dot(rows, weight_ref[...], preferred_element_type=jnp.float32)
        product = product.astype(jnp.bfloat16)
        for i in range(count):
            out_ref[i, place] = product[i * own : (i + 1) * own]


def per_device(
    queries,
    row_adapter,
    doc_keys,
    doc_values,
    patch_keys,
    patch_values,
    patch_block,
    patch_slot,
    out_weight,
):
    seqs = lax.axis_size("seq")
    groups = lax.axis_size("head")
    pairs = seqs // 2
    own, heads, width = queries.shape
    lines = own * heads
    seq_index = lax.axis_index("seq")
    side = lax.rem(seq_index, 2)
    adapter_ids = jnp.arange(HD, dtype=jnp.int32)
    levels = [[2 * level + at for level in range(pairs)] for at in range(2)]
    corners = [
        [head * seqs + 2 * level + at for head in range(groups) for at in (1, 0)]
        for level in range(pairs)
    ]

    def partner(array):
        return lax.ppermute(array, "seq", [(i, i ^ 1) for i in range(seqs)])

    def along_levels(array):
        return lax.all_to_all(array, "seq", 0, 0, tiled=True, axis_index_groups=levels)

    vmem = pltpu.CompilerParams(vmem_limit_bytes=VMEM)
    small = pltpu.CompilerParams(vmem_limit_bytes=16 * 2**20)

    def cost(flops, size):
        return pl.CostEstimate(flops=flops, bytes_accessed=size, transcendentals=0)

    part_shape = jax.ShapeDtypeStruct((pairs, lines + TAIL, width), jnp.bfloat16)
    own_shape = jax.ShapeDtypeStruct((1, lines + TAIL, width), jnp.bfloat16)

    message, own_message = pl.pallas_call(
        pack,
        in_specs=[
            pl.BlockSpec(memory_space=pltpu.VMEM),
            pl.BlockSpec(memory_space=pltpu.SMEM),
        ],
        out_shape=(part_shape, own_shape),
        compiler_params=pltpu.CompilerParams(vmem_limit_bytes=60 * 2**20),
        name="pack",
    )(queries, row_adapter)
    with jax.named_scope("gather_queries"):
        near = along_levels(message)
        far = partner(near)
    doc_len = doc_keys.shape[0]
    slots_here = patch_keys.shape[0]
    tokens = doc_len + slots_here * BLK
    in_vmem = pl.BlockSpec(memory_space=pltpu.VMEM)
    in_smem = pl.BlockSpec(memory_space=pltpu.SMEM)
    local = (
        doc_keys.reshape(doc_len, width),
        doc_values.reshape(doc_len, width),
        jnp.concatenate(
            [
                patch_keys.reshape(slots_here * BLK, width),
                patch_values.reshape(slots_here * BLK, width),
            ],
            0,
        ),
    )
    own_bars, first_bars, second_bars = pl.pallas_call(
        functools.partial(bar, slots_here),
        in_specs=[in_smem] + [in_vmem] * 5,
        out_shape=[jax.ShapeDtypeStruct((tokens // BLK, HD), jnp.float32)] * 3,
        compiler_params=small,
        cost_estimate=cost(10**7, 10**6),
        name="bar",
    )(seq_index.reshape(1), patch_block.reshape(1, -1), patch_slot.reshape(1, -1), *local)

    kept_shapes = (
        jax.ShapeDtypeStruct((pairs, lines, width), jnp.float32),
        jax.ShapeDtypeStruct((pairs, lines), jnp.float32),
    )

    def attend_lines(body, out_shape, messages, first_specs=()):
        return pl.pallas_call(
            body,
            in_specs=list(first_specs) + [in_vmem] * 5,
            out_shape=out_shape,
            compiler_params=vmem,
            cost_estimate=pl.CostEstimate(
                flops=8 * messages * lines * tokens * HD,
                bytes_accessed=4 * tokens * HD + 4 * messages * lines * width,
                transcendentals=messages * lines * tokens,
            ),
            name=body.__name__,
        )

    own_part = attend_lines(attend_own, own_shape, 1)(own_message, *local, own_bars)
    near_part = attend_lines(attend_rest, part_shape, pairs - 1, (in_smem, in_vmem))(
        (seq_index // 2).reshape(1), own_part, near, *local, first_bars
    )
    with jax.named_scope("swap_parts"):
        far_part = partner(near_part)
    mean, logsum = attend_lines(attend_kept, kept_shapes, pairs)(far, *local, second_bars)
    merged = pl.pallas_call(
        merge,
        out_shape=part_shape,
        compiler_params=small,
        cost_estimate=cost(10**6, 10**6),
        name="merge",
    )(mean, logsum, far_part)
    late_weight, merged = lax.optimization_barrier((out_weight, merged))
    other_weight = partner(late_weight)
    with jax.named_scope("scatter_rows"):
        parts = along_levels(merged)
    copies = pl.pallas_call(
        combine,
        out_shape=jax.ShapeDtypeStruct((pairs, own, heads * width), jnp.bfloat16),
        compiler_params=small,
        cost_estimate=cost(10**6, 10**6),
        name="combine",
    )(parts)
    with jax.named_scope("gather_attended"):
        attended = along_levels(copies)
    products = pl.pallas_call(
        project,
        in_specs=[in_smem] + [in_vmem] * 3,
        out_shape=jax.ShapeDtypeStruct((pairs, 2, own, out_weight.shape[1]), jnp.bfloat16),
        compiler_params=small,
        cost_estimate=cost(3 * 10**8, 2 * 10**6),
        name="project",
    )(side.reshape(1), attended, out_weight, other_weight)
    with jax.named_scope("sum_heads"):
        shares = lax.all_to_all(
            products.reshape(2 * pairs, own, out_weight.shape[1]),
            ("head", "seq"),
            0,
            0,
            tiled=True,
            axis_index_groups=corners,
        )
        shares = shares.reshape(groups, 2 * own, out_weight.shape[1])
        return jnp.sum(shares.astype(jnp.float32), axis=0)


def solution(mesh):
    placed = (
        P(("rows", "seq"), "head", None),
        P(("rows", "seq")),
        P("seq", "head", None),
        P("seq", "head", None),
        P("seq", None, "head", None),
        P("seq", None, "head", None),
        P(),
        P(),
        P("head", "seq"),
    )
    return jax.shard_map(
        per_device,
        mesh=mesh,
        in_specs=placed,
        out_specs=P(("rows", "head"), "seq"),
        check_vma=False,
    )
```

```python
import functools
import math

import jax
import jax.numpy as jnp
from jax import lax
from jax.experimental import pallas as pl
from jax.experimental.pallas import tpu as pltpu
from jax.sharding import PartitionSpec as P

BLK = 128
ADAPTERS = 64
PATCHES = 4
HD = 128
RATE = math.log2(math.e) / math.sqrt(HD)
HIDDEN = -1e30
TAIL = 16
SPAN = 512
OWN_SPAN = 2048
VMEM = 24 * 2**20


def pack(query_ref, adapter_ref, out_ref, own_ref):
    rows, heads, width = query_ref.shape
    query = query_ref[...].astype(jnp.float32)
    line = lax.broadcasted_iota(jnp.int32, (rows, width), 0)
    lane = lax.broadcasted_iota(jnp.int32, (rows, width), 1)
    onehot = jnp.zeros((rows, width), jnp.float32)
    for r in range(rows):
        onehot = jnp.where((line == r) & (lane == adapter_ref[r]), 1.0, onehot)
    lines = [query[:, h, :] for h in range(heads)] + [onehot]
    message = jnp.concatenate(lines, 0).astype(jnp.bfloat16)
    for i in range(out_ref.shape[0]):
        out_ref[i] = message
    own_ref[0] = message


def bar(slots, seq_ref, block_ref, slot_ref, *refs):
    bars_refs = refs[-3:]
    entries = block_ref.shape[1]
    blocks = bars_refs[0].shape[0] - slots
    line = lax.broadcasted_iota(jnp.int32, (blocks + slots, entries), 0)
    named = jnp.where(
        line < blocks,
        jnp.broadcast_to(block_ref[...], line.shape) - seq_ref[0] * blocks,
        jnp.broadcast_to(slot_ref[...], line.shape) - seq_ref[0] * slots + blocks,
    )
    entry = lax.broadcasted_iota(jnp.int32, (entries, HD), 0)
    adapter = lax.broadcasted_iota(jnp.int32, (entries, HD), 1)
    owns = jnp.where(entry // PATCHES == adapter, 1.0, 0.0).astype(jnp.bfloat16)
    hits = jnp.dot(
        jnp.where(named == line, 1.0, 0.0).astype(jnp.bfloat16),
        owns,
        preferred_element_type=jnp.float32,
    )
    is_block = lax.broadcasted_iota(jnp.int32, hits.shape, 0) < blocks
    hidden = jnp.where(is_block, hits, 1.0 - hits) > 0.5
    bars = jnp.where(hidden, HIDDEN, 0.0)
    for bars_ref in bars_refs:
        bars_ref[...] = bars


def store_part(out_ref, i, mean, logsum):
    lines = mean.shape[0]
    line = lax.broadcasted_iota(jnp.int32, (TAIL, lines), 0)
    out_ref[i, :lines, :] = mean.astype(jnp.bfloat16)
    flat = logsum
    first = flat.astype(jnp.bfloat16).astype(jnp.float32)
    second = (flat - first).astype(jnp.bfloat16).astype(jnp.float32)
    third = flat - first - second
    tail = jnp.where(
        line == 0, first, jnp.where(line == 1, second, jnp.where(line == 2, third, 0.0))
    )
    out_ref[i, lines:, :] = tail.astype(jnp.bfloat16)


def local_attention(places, span, msg_ref, doc_ref, doc_values_ref, patches_ref, bars_ref):
    lines = msg_ref.shape[1] - TAIL
    heads = lines // TAIL
    parts = []
    for i in places:
        onehot = msg_ref[i, lines:, :]
        parts.append(
            jnp.concatenate(
                [msg_ref[i, :lines, :], jnp.concatenate([onehot] * heads, 0)], 1
            )
        )
    query = jnp.concatenate(parts, 0)
    ones = jnp.ones((span, HD), jnp.bfloat16)
    peak = accum = None
    bar = 0
    patch_len = patches_ref.shape[0] // 2
    patch_ref = patches_ref.at[pl.ds(0, patch_len)]
    patch_values_ref = patches_ref.at[pl.ds(patch_len, patch_len)]
    for keys_ref, values_ref in ((doc_ref, doc_values_ref), (patch_ref, patch_values_ref)):
        for start in range(0, keys_ref.shape[0], span):
            bars = []
            for _ in range(span // BLK):
                tile = jnp.broadcast_to(bars_ref[bar : bar + 1, :], (TAIL, HD))
                bars += [tile.astype(jnp.bfloat16)] * (BLK // TAIL)
                bar += 1
            keys = jnp.concatenate(
                [keys_ref[start : start + span, :], jnp.concatenate(bars, 0)], 1
            )
            values = jnp.concatenate([values_ref[start : start + span, :], ones], 1)
            scores = lax.dot_general(
                query, keys, (((1,), (1,)), ((), ())), preferred_element_type=jnp.float32
            )
            top = jnp.max(scores, axis=1, keepdims=True)
            if accum is not None:
                top = jnp.maximum(peak, top)
            weights = jnp.exp2((scores - top) * RATE).astype(jnp.bfloat16)
            added = jnp.dot(weights, values, preferred_element_type=jnp.float32)
            accum = added if accum is None else accum * jnp.exp2((peak - top) * RATE) + added
            peak = top
    total = accum[:, HD:]
    mean = accum[:, :HD] / total
    return mean, peak * RATE + jnp.log2(total)


def attend_own(msg_ref, *refs):
    *local, out_ref = refs
    send(range(msg_ref.shape[0]), OWN_SPAN, msg_ref, local, out_ref)


def attend_rest(level_ref, own_ref, msg_ref, *refs):
    *local, out_ref = refs
    count = msg_ref.shape[0]
    out_ref[level_ref[0]] = own_ref[0]
    places = [lax.rem(level_ref[0] + i, count) for i in range(1, count)]
    send(places, SPAN, msg_ref, local, out_ref)


def send(places, span, msg_ref, local, out_ref):
    mean, logsum = local_attention(places, span, msg_ref, *local)
    lines = msg_ref.shape[1] - TAIL
    for i, place in enumerate(places):
        store_part(
            out_ref,
            place,
            mean[i * lines : (i + 1) * lines],
            jnp.transpose(logsum[i * lines : (i + 1) * lines])[:TAIL, :],
        )


def attend_kept(_, msg_ref, *refs):
    *local, mean_ref, logsum_ref = refs
    mean, logsum = local_attention(range(msg_ref.shape[0]), SPAN, msg_ref, *local)
    lines = msg_ref.shape[1] - TAIL
    for i in range(msg_ref.shape[0]):
        mean_ref[i] = mean[i * lines : (i + 1) * lines]
        logsum_ref[i : i + 1, :] = jnp.transpose(logsum[i * lines : (i + 1) * lines])[:1, :]


def columns(flat, lines):
    count = flat.shape[0]
    return jnp.transpose(
        jnp.concatenate([flat, jnp.zeros((lines - count, lines), jnp.float32)], 0)
    )


def merge(mean_ref, logsum_ref, two_ref, out_ref):
    count = two_ref.shape[0]
    lines = two_ref.shape[1] - TAIL
    one = logsum_ref[...]
    two = jnp.sum(two_ref[:, lines:, :].astype(jnp.float32), axis=1)
    top = jnp.maximum(one, two)
    first, second = jnp.exp2(one - top), jnp.exp2(two - top)
    both = first + second
    shares = columns(jnp.concatenate([first / both, second / both], 0), lines)
    logsum = top + jnp.log2(both)
    for i in range(count):
        mean = (
            mean_ref[i] * shares[:, i : i + 1]
            + two_ref[i, :lines, :].astype(jnp.float32) * shares[:, count + i : count + i + 1]
        )
        store_part(out_ref, i, mean, jnp.broadcast_to(logsum[i : i + 1, :], (TAIL, lines)))


def combine(parts_ref, out_ref):
    count = parts_ref.shape[0]
    lines = parts_ref.shape[1] - TAIL
    heads = lines // TAIL
    logsum = jnp.sum(parts_ref[:, lines:, :].astype(jnp.float32), axis=1)
    share = jnp.exp2(logsum - jnp.max(logsum, axis=0, keepdims=True))
    share = columns(share / jnp.sum(share, axis=0, keepdims=True), lines)
    mixed = None
    for i in range(count):
        term = parts_ref[i, :lines, :].astype(jnp.float32) * share[:, i : i + 1]
        mixed = term if mixed is None else mixed + term
    attended = mixed.astype(jnp.bfloat16)
    wide = jnp.concatenate([attended[h * TAIL : (h + 1) * TAIL] for h in range(heads)], 1)
    for i in range(out_ref.shape[0]):
        out_ref[i] = wide


def project(side_ref, rows_ref, own_ref, other_ref, out_ref):
    side = side_ref[0]
    count, own = rows_ref.shape[0], rows_ref.shape[1]
    rows = jnp.concatenate([rows_ref[i] for i in range(count)], 0)
    for weight_ref, place in ((own_ref, 1 - side), (other_ref, side)):
        product = jnp.dot(rows, weight_ref[...], preferred_element_type=jnp.float32)
        product = product.astype(jnp.bfloat16)
        for i in range(count):
            out_ref[i, place] = product[i * own : (i + 1) * own]


def per_device(
    queries,
    row_adapter,
    doc_keys,
    doc_values,
    patch_keys,
    patch_values,
    patch_block,
    patch_slot,
    out_weight,
):
    seqs = lax.axis_size("seq")
    groups = lax.axis_size("head")
    pairs = seqs // 2
    own, heads, width = queries.shape
    lines = own * heads
    seq_index = lax.axis_index("seq")
    side = lax.rem(seq_index, 2)
    adapter_ids = jnp.arange(HD, dtype=jnp.int32)
    levels = [[2 * level + at for level in range(pairs)] for at in range(2)]
    corners = [
        [head * seqs + 2 * level + at for head in range(groups) for at in (1, 0)]
        for level in range(pairs)
    ]

    def partner(array):
        return lax.ppermute(array, "seq", [(i, i ^ 1) for i in range(seqs)])

    def along_levels(array):
        return lax.all_to_all(array, "seq", 0, 0, tiled=True, axis_index_groups=levels)

    vmem = pltpu.CompilerParams(vmem_limit_bytes=VMEM)
    small = pltpu.CompilerParams(vmem_limit_bytes=16 * 2**20)

    def cost(flops, size):
        return pl.CostEstimate(flops=flops, bytes_accessed=size, transcendentals=0)

    part_shape = jax.ShapeDtypeStruct((pairs, lines + TAIL, width), jnp.bfloat16)
    own_shape = jax.ShapeDtypeStruct((1, lines + TAIL, width), jnp.bfloat16)

    message, own_message = pl.pallas_call(
        pack,
        in_specs=[
            pl.BlockSpec(memory_space=pltpu.VMEM),
            pl.BlockSpec(memory_space=pltpu.SMEM),
        ],
        out_shape=(part_shape, own_shape),
        compiler_params=pltpu.CompilerParams(vmem_limit_bytes=60 * 2**20),
        name="pack",
    )(queries, row_adapter)
    with jax.named_scope("gather_queries"):
        near = along_levels(message)
        far = partner(near)
    doc_len = doc_keys.shape[0]
    slots_here = patch_keys.shape[0]
    tokens = doc_len + slots_here * BLK
    in_vmem = pl.BlockSpec(memory_space=pltpu.VMEM)
    in_smem = pl.BlockSpec(memory_space=pltpu.SMEM)
    local = (
        doc_keys.reshape(doc_len, width),
        doc_values.reshape(doc_len, width),
        jnp.concatenate(
            [
                patch_keys.reshape(slots_here * BLK, width),
                patch_values.reshape(slots_here * BLK, width),
            ],
            0,
        ),
    )
    own_bars, first_bars, second_bars = pl.pallas_call(
        functools.partial(bar, slots_here),
        in_specs=[in_smem] + [in_vmem] * 5,
        out_shape=[jax.ShapeDtypeStruct((tokens // BLK, HD), jnp.float32)] * 3,
        compiler_params=small,
        cost_estimate=cost(10**7, 10**6),
        name="bar",
    )(seq_index.reshape(1), patch_block.reshape(1, -1), patch_slot.reshape(1, -1), *local)

    kept_shapes = (
        jax.ShapeDtypeStruct((pairs, lines, width), jnp.float32),
        jax.ShapeDtypeStruct((pairs, lines), jnp.float32),
    )

    def attend_lines(body, out_shape, messages, first_specs=()):
        return pl.pallas_call(
            body,
            in_specs=list(first_specs) + [in_vmem] * 5,
            out_shape=out_shape,
            compiler_params=vmem,
            cost_estimate=pl.CostEstimate(
                flops=8 * messages * lines * tokens * HD,
                bytes_accessed=4 * tokens * HD + 4 * messages * lines * width,
                transcendentals=messages * lines * tokens,
            ),
            name=body.__name__,
        )

    own_part = attend_lines(attend_own, own_shape, 1)(own_message, *local, own_bars)
    near_part = attend_lines(attend_rest, part_shape, pairs - 1, (in_smem, in_vmem))(
        (seq_index // 2).reshape(1), own_part, near, *local, first_bars
    )
    with jax.named_scope("swap_parts"):
        far_part = partner(near_part)
    mean, logsum = attend_lines(attend_kept, kept_shapes, pairs, (in_vmem,))(
        out_weight, far, *local, second_bars
    )
    merged = pl.pallas_call(
        merge,
        out_shape=part_shape,
        compiler_params=small,
        cost_estimate=cost(10**6, 10**6),
        name="merge",
    )(mean, logsum, far_part)
    late_weight, merged = lax.optimization_barrier((out_weight, merged))
    other_weight = partner(late_weight)
    with jax.named_scope("scatter_rows"):
        parts = along_levels(merged)
    copies = pl.pallas_call(
        combine,
        out_shape=jax.ShapeDtypeStruct((pairs, own, heads * width), jnp.bfloat16),
        compiler_params=small,
        cost_estimate=cost(10**6, 10**6),
        name="combine",
    )(parts)
    with jax.named_scope("gather_attended"):
        attended = along_levels(copies)
    products = pl.pallas_call(
        project,
        in_specs=[in_smem] + [in_vmem] * 3,
        out_shape=jax.ShapeDtypeStruct((pairs, 2, own, out_weight.shape[1]), jnp.bfloat16),
        compiler_params=small,
        cost_estimate=cost(3 * 10**8, 2 * 10**6),
        name="project",
    )(side.reshape(1), attended, out_weight, other_weight)
    with jax.named_scope("sum_heads"):
        shares = lax.all_to_all(
            products.reshape(2 * pairs, own, out_weight.shape[1]),
            ("head", "seq"),
            0,
            0,
            tiled=True,
            axis_index_groups=corners,
        )
        shares = shares.reshape(groups, 2 * own, out_weight.shape[1])
        return jnp.sum(shares.astype(jnp.float32), axis=0)


def solution(mesh):
    placed = (
        P(("rows", "seq"), "head", None),
        P(("rows", "seq")),
        P("seq", "head", None),
        P("seq", "head", None),
        P("seq", None, "head", None),
        P("seq", None, "head", None),
        P(),
        P(),
        P("head", "seq"),
    )
    return jax.shard_map(
        per_device,
        mesh=mesh,
        in_specs=placed,
        out_specs=P(("rows", "head"), "seq"),
        check_vma=False,
    )
```

```python
import functools
import math

import jax
import jax.numpy as jnp
from jax import lax
from jax.experimental import pallas as pl
from jax.experimental.pallas import tpu as pltpu
from jax.sharding import PartitionSpec as P

BLK = 128
ADAPTERS = 64
PATCHES = 4
HD = 128
RATE = math.log2(math.e) / math.sqrt(HD)
HIDDEN = -1e30
TAIL = 16
SPAN = 512
OWN_SPAN = 2048
VMEM = 24 * 2**20


def pack(query_ref, adapter_ref, out_ref, own_ref):
    rows, heads, width = query_ref.shape
    query = query_ref[...].astype(jnp.float32)
    line = lax.broadcasted_iota(jnp.int32, (rows, width), 0)
    lane = lax.broadcasted_iota(jnp.int32, (rows, width), 1)
    onehot = jnp.zeros((rows, width), jnp.float32)
    for r in range(rows):
        onehot = jnp.where((line == r) & (lane == adapter_ref[r]), 1.0, onehot)
    lines = [query[:, h, :] for h in range(heads)] + [onehot]
    message = jnp.concatenate(lines, 0).astype(jnp.bfloat16)
    for i in range(out_ref.shape[0]):
        out_ref[i] = message
    own_ref[0] = message


def bar(slots, seq_ref, block_ref, slot_ref, *refs):
    bars_refs = refs[-4:]
    entries = block_ref.shape[1]
    blocks = bars_refs[0].shape[0] - slots
    line = lax.broadcasted_iota(jnp.int32, (blocks + slots, entries), 0)
    named = jnp.where(
        line < blocks,
        jnp.broadcast_to(block_ref[...], line.shape) - seq_ref[0] * blocks,
        jnp.broadcast_to(slot_ref[...], line.shape) - seq_ref[0] * slots + blocks,
    )
    entry = lax.broadcasted_iota(jnp.int32, (entries, HD), 0)
    adapter = lax.broadcasted_iota(jnp.int32, (entries, HD), 1)
    owns = jnp.where(entry // PATCHES == adapter, 1.0, 0.0).astype(jnp.bfloat16)
    hits = jnp.dot(
        jnp.where(named == line, 1.0, 0.0).astype(jnp.bfloat16),
        owns,
        preferred_element_type=jnp.float32,
    )
    is_block = lax.broadcasted_iota(jnp.int32, hits.shape, 0) < blocks
    hidden = jnp.where(is_block, hits, 1.0 - hits) > 0.5
    bars = jnp.where(hidden, HIDDEN, 0.0)
    for bars_ref in bars_refs:
        bars_ref[...] = bars


def store_part(out_ref, i, mean, logsum):
    lines = mean.shape[0]
    line = lax.broadcasted_iota(jnp.int32, (TAIL, lines), 0)
    out_ref[i, :lines, :] = mean.astype(jnp.bfloat16)
    flat = logsum
    first = flat.astype(jnp.bfloat16).astype(jnp.float32)
    second = (flat - first).astype(jnp.bfloat16).astype(jnp.float32)
    third = flat - first - second
    tail = jnp.where(
        line == 0, first, jnp.where(line == 1, second, jnp.where(line == 2, third, 0.0))
    )
    out_ref[i, lines:, :] = tail.astype(jnp.bfloat16)


def local_attention(places, span, msg_ref, doc_ref, doc_values_ref, patches_ref, bars_ref):
    lines = msg_ref.shape[1] - TAIL
    heads = lines // TAIL
    parts = []
    for i in places:
        onehot = msg_ref[i, lines:, :]
        parts.append(
            jnp.concatenate(
                [msg_ref[i, :lines, :], jnp.concatenate([onehot] * heads, 0)], 1
            )
        )
    query = jnp.concatenate(parts, 0)
    ones = jnp.ones((span, HD), jnp.bfloat16)
    peak = accum = None
    bar = 0
    patch_len = patches_ref.shape[0] // 2
    patch_ref = patches_ref.at[pl.ds(0, patch_len)]
    patch_values_ref = patches_ref.at[pl.ds(patch_len, patch_len)]
    for keys_ref, values_ref in ((doc_ref, doc_values_ref), (patch_ref, patch_values_ref)):
        for start in range(0, keys_ref.shape[0], span):
            bars = []
            for _ in range(span // BLK):
                tile = jnp.broadcast_to(bars_ref[bar : bar + 1, :], (TAIL, HD))
                bars += [tile.astype(jnp.bfloat16)] * (BLK // TAIL)
                bar += 1
            keys = jnp.concatenate(
                [keys_ref[start : start + span, :], jnp.concatenate(bars, 0)], 1
            )
            values = jnp.concatenate([values_ref[start : start + span, :], ones], 1)
            scores = lax.dot_general(
                query, keys, (((1,), (1,)), ((), ())), preferred_element_type=jnp.float32
            )
            top = jnp.max(scores, axis=1, keepdims=True)
            if accum is not None:
                top = jnp.maximum(peak, top)
            weights = jnp.exp2((scores - top) * RATE).astype(jnp.bfloat16)
            added = jnp.dot(weights, values, preferred_element_type=jnp.float32)
            accum = added if accum is None else accum * jnp.exp2((peak - top) * RATE) + added
            peak = top
    total = accum[:, HD:]
    mean = accum[:, :HD] / total
    return mean, peak * RATE + jnp.log2(total)


def attend_own(msg_ref, *refs):
    *local, out_ref = refs
    send(range(msg_ref.shape[0]), OWN_SPAN, msg_ref, local, out_ref)


def attend_rest(level_ref, own_ref, msg_ref, *refs):
    *local, out_ref = refs
    count = msg_ref.shape[0]
    out_ref[level_ref[0]] = own_ref[0]
    places = [lax.rem(level_ref[0] + i, count) for i in range(1, count)]
    send(places, SPAN, msg_ref, local, out_ref)


def send(places, span, msg_ref, local, out_ref):
    mean, logsum = local_attention(places, span, msg_ref, *local)
    lines = msg_ref.shape[1] - TAIL
    for i, place in enumerate(places):
        store_part(
            out_ref,
            place,
            mean[i * lines : (i + 1) * lines],
            jnp.transpose(logsum[i * lines : (i + 1) * lines])[:TAIL, :],
        )


def keep(places, span, msg_ref, local, mean_ref, logsum_ref):
    mean, logsum = local_attention(places, span, msg_ref, *local)
    lines = msg_ref.shape[1] - TAIL
    for i, place in enumerate(places):
        mean_ref[place] = mean[i * lines : (i + 1) * lines]
        logsum_ref[pl.ds(place, 1), :] = jnp.transpose(logsum[i * lines : (i + 1) * lines])[:1, :]


def attend_early(msg_ref, *refs):
    *local, mean_ref, logsum_ref = refs
    keep([0], OWN_SPAN, msg_ref, local, mean_ref, logsum_ref)


def attend_kept(level_ref, _, early_mean_ref, early_logsum_ref, msg_ref, *refs):
    *local, mean_ref, logsum_ref = refs
    count = msg_ref.shape[0]
    level = level_ref[0]
    mean_ref[level] = early_mean_ref[0]
    logsum_ref[pl.ds(level, 1), :] = early_logsum_ref[...]
    places = [lax.rem(level + i, count) for i in range(1, count)]
    keep(places, SPAN, msg_ref, local, mean_ref, logsum_ref)


def columns(flat, lines):
    count = flat.shape[0]
    return jnp.transpose(
        jnp.concatenate([flat, jnp.zeros((lines - count, lines), jnp.float32)], 0)
    )


def merge(mean_ref, logsum_ref, two_ref, out_ref):
    count = two_ref.shape[0]
    lines = two_ref.shape[1] - TAIL
    one = logsum_ref[...]
    two = jnp.sum(two_ref[:, lines:, :].astype(jnp.float32), axis=1)
    top = jnp.maximum(one, two)
    first, second = jnp.exp2(one - top), jnp.exp2(two - top)
    both = first + second
    shares = columns(jnp.concatenate([first / both, second / both], 0), lines)
    logsum = top + jnp.log2(both)
    for i in range(count):
        mean = (
            mean_ref[i] * shares[:, i : i + 1]
            + two_ref[i, :lines, :].astype(jnp.float32) * shares[:, count + i : count + i + 1]
        )
        store_part(out_ref, i, mean, jnp.broadcast_to(logsum[i : i + 1, :], (TAIL, lines)))


def combine(parts_ref, out_ref):
    count = parts_ref.shape[0]
    lines = parts_ref.shape[1] - TAIL
    heads = lines // TAIL
    logsum = jnp.sum(parts_ref[:, lines:, :].astype(jnp.float32), axis=1)
    share = jnp.exp2(logsum - jnp.max(logsum, axis=0, keepdims=True))
    share = columns(share / jnp.sum(share, axis=0, keepdims=True), lines)
    mixed = None
    for i in range(count):
        term = parts_ref[i, :lines, :].astype(jnp.float32) * share[:, i : i + 1]
        mixed = term if mixed is None else mixed + term
    attended = mixed.astype(jnp.bfloat16)
    wide = jnp.concatenate([attended[h * TAIL : (h + 1) * TAIL] for h in range(heads)], 1)
    for i in range(out_ref.shape[0]):
        out_ref[i] = wide


def project(side_ref, rows_ref, own_ref, other_ref, out_ref):
    side = side_ref[0]
    count, own = rows_ref.shape[0], rows_ref.shape[1]
    rows = jnp.concatenate([rows_ref[i] for i in range(count)], 0)
    for weight_ref, place in ((own_ref, 1 - side), (other_ref, side)):
        product = jnp.dot(rows, weight_ref[...], preferred_element_type=jnp.float32)
        product = product.astype(jnp.bfloat16)
        for i in range(count):
            out_ref[i, place] = product[i * own : (i + 1) * own]


def per_device(
    queries,
    row_adapter,
    doc_keys,
    doc_values,
    patch_keys,
    patch_values,
    patch_block,
    patch_slot,
    out_weight,
):
    seqs = lax.axis_size("seq")
    groups = lax.axis_size("head")
    pairs = seqs // 2
    own, heads, width = queries.shape
    lines = own * heads
    seq_index = lax.axis_index("seq")
    side = lax.rem(seq_index, 2)
    adapter_ids = jnp.arange(HD, dtype=jnp.int32)
    levels = [[2 * level + at for level in range(pairs)] for at in range(2)]
    corners = [
        [head * seqs + 2 * level + at for head in range(groups) for at in (1, 0)]
        for level in range(pairs)
    ]

    def partner(array):
        return lax.ppermute(array, "seq", [(i, i ^ 1) for i in range(seqs)])

    def along_levels(array):
        return lax.all_to_all(array, "seq", 0, 0, tiled=True, axis_index_groups=levels)

    vmem = pltpu.CompilerParams(vmem_limit_bytes=VMEM)
    small = pltpu.CompilerParams(vmem_limit_bytes=16 * 2**20)

    def cost(flops, size):
        return pl.CostEstimate(flops=flops, bytes_accessed=size, transcendentals=0)

    part_shape = jax.ShapeDtypeStruct((pairs, lines + TAIL, width), jnp.bfloat16)
    own_shape = jax.ShapeDtypeStruct((1, lines + TAIL, width), jnp.bfloat16)

    message, own_message = pl.pallas_call(
        pack,
        in_specs=[
            pl.BlockSpec(memory_space=pltpu.VMEM),
            pl.BlockSpec(memory_space=pltpu.SMEM),
        ],
        out_shape=(part_shape, own_shape),
        compiler_params=pltpu.CompilerParams(vmem_limit_bytes=60 * 2**20),
        name="pack",
    )(queries, row_adapter)
    early_message = partner(own_message)
    with jax.named_scope("gather_queries"):
        near = along_levels(message)
        far = partner(near)
    doc_len = doc_keys.shape[0]
    slots_here = patch_keys.shape[0]
    tokens = doc_len + slots_here * BLK
    in_vmem = pl.BlockSpec(memory_space=pltpu.VMEM)
    in_smem = pl.BlockSpec(memory_space=pltpu.SMEM)
    local = (
        doc_keys.reshape(doc_len, width),
        doc_values.reshape(doc_len, width),
        jnp.concatenate(
            [
                patch_keys.reshape(slots_here * BLK, width),
                patch_values.reshape(slots_here * BLK, width),
            ],
            0,
        ),
    )
    own_bars, early_bars, first_bars, second_bars = pl.pallas_call(
        functools.partial(bar, slots_here),
        in_specs=[in_smem] + [in_vmem] * 5,
        out_shape=[jax.ShapeDtypeStruct((tokens // BLK, HD), jnp.float32)] * 4,
        compiler_params=small,
        cost_estimate=cost(10**7, 10**6),
        name="bar",
    )(seq_index.reshape(1), patch_block.reshape(1, -1), patch_slot.reshape(1, -1), *local)

    kept_shapes = (
        jax.ShapeDtypeStruct((pairs, lines, width), jnp.float32),
        jax.ShapeDtypeStruct((pairs, lines), jnp.float32),
    )

    def attend_lines(body, out_shape, messages, first_specs=()):
        return pl.pallas_call(
            body,
            in_specs=list(first_specs) + [in_vmem] * 5,
            out_shape=out_shape,
            compiler_params=vmem,
            cost_estimate=pl.CostEstimate(
                flops=8 * messages * lines * tokens * HD,
                bytes_accessed=4 * tokens * HD + 4 * messages * lines * width,
                transcendentals=messages * lines * tokens,
            ),
            name=body.__name__,
        )

    own_part = attend_lines(attend_own, own_shape, 1)(own_message, *local, own_bars)
    early_shapes = tuple(
        jax.ShapeDtypeStruct((1, *shape.shape[1:]), shape.dtype) for shape in kept_shapes
    )
    early = attend_lines(attend_early, early_shapes, 1)(early_message, *local, early_bars)
    near, *early = lax.optimization_barrier((near, *early))
    level = (seq_index // 2).reshape(1)
    near_part = attend_lines(attend_rest, part_shape, pairs - 1, (in_smem, in_vmem))(
        level, own_part, near, *local, first_bars
    )
    with jax.named_scope("swap_parts"):
        far_part = partner(near_part)
    mean, logsum = attend_lines(attend_kept, kept_shapes, pairs - 1, (in_smem,) + (in_vmem,) * 3)(
        level, out_weight, *early, far, *local, second_bars
    )
    merged = pl.pallas_call(
        merge,
        out_shape=part_shape,
        compiler_params=small,
        cost_estimate=cost(10**6, 10**6),
        name="merge",
    )(mean, logsum, far_part)
    late_weight, merged = lax.optimization_barrier((out_weight, merged))
    other_weight = partner(late_weight)
    with jax.named_scope("scatter_rows"):
        parts = along_levels(merged)
    copies = pl.pallas_call(
        combine,
        out_shape=jax.ShapeDtypeStruct((pairs, own, heads * width), jnp.bfloat16),
        compiler_params=small,
        cost_estimate=cost(10**6, 10**6),
        name="combine",
    )(parts)
    with jax.named_scope("gather_attended"):
        attended = along_levels(copies)
    products = pl.pallas_call(
        project,
        in_specs=[in_smem] + [in_vmem] * 3,
        out_shape=jax.ShapeDtypeStruct((pairs, 2, own, out_weight.shape[1]), jnp.bfloat16),
        compiler_params=small,
        cost_estimate=cost(3 * 10**8, 2 * 10**6),
        name="project",
    )(side.reshape(1), attended, out_weight, other_weight)
    with jax.named_scope("sum_heads"):
        shares = lax.all_to_all(
            products.reshape(2 * pairs, own, out_weight.shape[1]),
            ("head", "seq"),
            0,
            0,
            tiled=True,
            axis_index_groups=corners,
        )
        shares = shares.reshape(groups, 2 * own, out_weight.shape[1])
        return jnp.sum(shares.astype(jnp.float32), axis=0)


def solution(mesh):
    placed = (
        P(("rows", "seq"), "head", None),
        P(("rows", "seq")),
        P("seq", "head", None),
        P("seq", "head", None),
        P("seq", None, "head", None),
        P("seq", None, "head", None),
        P(),
        P(),
        P("head", "seq"),
    )
    return jax.shard_map(
        per_device,
        mesh=mesh,
        in_specs=placed,
        out_specs=P(("rows", "head"), "seq"),
        check_vma=False,
    )
```

```python
import functools
import math

import jax
import jax.numpy as jnp
from jax import lax
from jax.experimental import pallas as pl
from jax.experimental.pallas import tpu as pltpu
from jax.sharding import PartitionSpec as P

BLK = 128
ADAPTERS = 64
PATCHES = 4
HD = 128
RATE = math.log2(math.e) / math.sqrt(HD)
HIDDEN = -1e30
TAIL = 16
SPAN = 512
OWN_SPAN = 2048
VMEM = 24 * 2**20


def pack(query_ref, adapter_ref, out_ref, own_ref):
    rows, heads, width = query_ref.shape
    query = query_ref[...].astype(jnp.float32)
    line = lax.broadcasted_iota(jnp.int32, (rows, width), 0)
    lane = lax.broadcasted_iota(jnp.int32, (rows, width), 1)
    onehot = jnp.zeros((rows, width), jnp.float32)
    for r in range(rows):
        onehot = jnp.where((line == r) & (lane == adapter_ref[r]), 1.0, onehot)
    lines = [query[:, h, :] for h in range(heads)] + [onehot]
    message = jnp.concatenate(lines, 0).astype(jnp.bfloat16)
    for i in range(out_ref.shape[0]):
        out_ref[i] = message
    own_ref[0] = message


def bar(slots, seq_ref, block_ref, slot_ref, *refs):
    bars_refs = refs[-3:]
    entries = block_ref.shape[1]
    blocks = bars_refs[0].shape[0] - slots
    line = lax.broadcasted_iota(jnp.int32, (blocks + slots, entries), 0)
    named = jnp.where(
        line < blocks,
        jnp.broadcast_to(block_ref[...], line.shape) - seq_ref[0] * blocks,
        jnp.broadcast_to(slot_ref[...], line.shape) - seq_ref[0] * slots + blocks,
    )
    entry = lax.broadcasted_iota(jnp.int32, (entries, HD), 0)
    adapter = lax.broadcasted_iota(jnp.int32, (entries, HD), 1)
    owns = jnp.where(entry // PATCHES == adapter, 1.0, 0.0).astype(jnp.bfloat16)
    hits = jnp.dot(
        jnp.where(named == line, 1.0, 0.0).astype(jnp.bfloat16),
        owns,
        preferred_element_type=jnp.float32,
    )
    is_block = lax.broadcasted_iota(jnp.int32, hits.shape, 0) < blocks
    hidden = jnp.where(is_block, hits, 1.0 - hits) > 0.5
    bars = jnp.where(hidden, HIDDEN, 0.0)
    for bars_ref in bars_refs:
        bars_ref[...] = bars


def store_part(out_ref, i, mean, logsum):
    lines = mean.shape[0]
    line = lax.broadcasted_iota(jnp.int32, (TAIL, lines), 0)
    out_ref[i, :lines, :] = mean.astype(jnp.bfloat16)
    flat = logsum
    first = flat.astype(jnp.bfloat16).astype(jnp.float32)
    second = (flat - first).astype(jnp.bfloat16).astype(jnp.float32)
    third = flat - first - second
    tail = jnp.where(
        line == 0, first, jnp.where(line == 1, second, jnp.where(line == 2, third, 0.0))
    )
    out_ref[i, lines:, :] = tail.astype(jnp.bfloat16)


def local_attention(places, span, msg_ref, doc_ref, doc_values_ref, patches_ref, bars_ref):
    lines = msg_ref.shape[1] - TAIL
    heads = lines // TAIL
    parts = []
    for i in places:
        onehot = msg_ref[i, lines:, :]
        parts.append(
            jnp.concatenate(
                [msg_ref[i, :lines, :], jnp.concatenate([onehot] * heads, 0)], 1
            )
        )
    query = jnp.concatenate(parts, 0)
    ones = jnp.ones((span, HD), jnp.bfloat16)
    peak = accum = None
    bar = 0
    patch_len = patches_ref.shape[0] // 2
    patch_ref = patches_ref.at[pl.ds(0, patch_len)]
    patch_values_ref = patches_ref.at[pl.ds(patch_len, patch_len)]
    for keys_ref, values_ref in ((doc_ref, doc_values_ref), (patch_ref, patch_values_ref)):
        for start in range(0, keys_ref.shape[0], span):
            bars = []
            for _ in range(span // BLK):
                tile = jnp.broadcast_to(bars_ref[bar : bar + 1, :], (TAIL, HD))
                bars += [tile.astype(jnp.bfloat16)] * (BLK // TAIL)
                bar += 1
            keys = jnp.concatenate(
                [keys_ref[start : start + span, :], jnp.concatenate(bars, 0)], 1
            )
            values = jnp.concatenate([values_ref[start : start + span, :], ones], 1)
            scores = lax.dot_general(
                query, keys, (((1,), (1,)), ((), ())), preferred_element_type=jnp.float32
            )
            top = jnp.max(scores, axis=1, keepdims=True)
            if accum is not None:
                top = jnp.maximum(peak, top)
            weights = jnp.exp2((scores - top) * RATE).astype(jnp.bfloat16)
            added = jnp.dot(weights, values, preferred_element_type=jnp.float32)
            accum = added if accum is None else accum * jnp.exp2((peak - top) * RATE) + added
            peak = top
    total = accum[:, HD:]
    mean = accum[:, :HD] / total
    return mean, peak * RATE + jnp.log2(total)


def attend_own(msg_ref, *refs):
    *local, out_ref = refs
    send(range(msg_ref.shape[0]), OWN_SPAN, msg_ref, local, out_ref)


def attend_rest(level_ref, own_ref, msg_ref, *refs):
    *local, out_ref = refs
    count = msg_ref.shape[0]
    out_ref[level_ref[0]] = own_ref[0]
    places = [lax.rem(level_ref[0] + i, count) for i in range(1, count)]
    send(places, SPAN, msg_ref, local, out_ref)


def send(places, span, msg_ref, local, out_ref):
    mean, logsum = local_attention(places, span, msg_ref, *local)
    lines = msg_ref.shape[1] - TAIL
    for i, place in enumerate(places):
        store_part(
            out_ref,
            place,
            mean[i * lines : (i + 1) * lines],
            jnp.transpose(logsum[i * lines : (i + 1) * lines])[:TAIL, :],
        )


def attend_kept(_, msg_ref, *refs):
    *local, mean_ref, logsum_ref = refs
    mean, logsum = local_attention(range(msg_ref.shape[0]), SPAN, msg_ref, *local)
    lines = msg_ref.shape[1] - TAIL
    for i in range(msg_ref.shape[0]):
        mean_ref[i] = mean[i * lines : (i + 1) * lines]
        logsum_ref[i : i + 1, :] = jnp.transpose(logsum[i * lines : (i + 1) * lines])[:1, :]


def columns(flat, lines):
    count = flat.shape[0]
    return jnp.transpose(
        jnp.concatenate([flat, jnp.zeros((lines - count, lines), jnp.float32)], 0)
    )


def merge(mean_ref, logsum_ref, two_ref, out_ref):
    count = two_ref.shape[0]
    lines = two_ref.shape[1] - TAIL
    one = logsum_ref[...]
    two = jnp.sum(two_ref[:, lines:, :].astype(jnp.float32), axis=1)
    top = jnp.maximum(one, two)
    first, second = jnp.exp2(one - top), jnp.exp2(two - top)
    both = first + second
    shares = columns(jnp.concatenate([first / both, second / both], 0), lines)
    logsum = top + jnp.log2(both)
    for i in range(count):
        mean = (
            mean_ref[i] * shares[:, i : i + 1]
            + two_ref[i, :lines, :].astype(jnp.float32) * shares[:, count + i : count + i + 1]
        )
        store_part(out_ref, i, mean, jnp.broadcast_to(logsum[i : i + 1, :], (TAIL, lines)))


def combine(parts_ref, out_ref):
    count = parts_ref.shape[0]
    lines = parts_ref.shape[1] - TAIL
    heads = lines // TAIL
    logsum = jnp.sum(parts_ref[:, lines:, :].astype(jnp.float32), axis=1)
    share = jnp.exp2(logsum - jnp.max(logsum, axis=0, keepdims=True))
    share = columns(share / jnp.sum(share, axis=0, keepdims=True), lines)
    mixed = None
    for i in range(count):
        term = parts_ref[i, :lines, :].astype(jnp.float32) * share[:, i : i + 1]
        mixed = term if mixed is None else mixed + term
    attended = mixed.astype(jnp.bfloat16)
    wide = jnp.concatenate([attended[h * TAIL : (h + 1) * TAIL] for h in range(heads)], 1)
    for i in range(out_ref.shape[0]):
        out_ref[i] = wide


def project(side_ref, rows_ref, own_ref, other_ref, out_ref):
    side = side_ref[0]
    count, own = rows_ref.shape[0], rows_ref.shape[1]
    rows = jnp.concatenate([rows_ref[i] for i in range(count)], 0)
    for weight_ref, place in ((own_ref, 1 - side), (other_ref, side)):
        product = jnp.dot(rows, weight_ref[...], preferred_element_type=jnp.float32)
        product = product.astype(jnp.bfloat16)
        for i in range(count):
            out_ref[i, place] = product[i * own : (i + 1) * own]


def add_shares(shares_ref, out_ref):
    total = shares_ref[0].astype(jnp.float32)
    for i in range(1, shares_ref.shape[0]):
        total = total + shares_ref[i].astype(jnp.float32)
    out_ref[...] = total


def per_device(
    queries,
    row_adapter,
    doc_keys,
    doc_values,
    patch_keys,
    patch_values,
    patch_block,
    patch_slot,
    out_weight,
):
    seqs = lax.axis_size("seq")
    groups = lax.axis_size("head")
    pairs = seqs // 2
    own, heads, width = queries.shape
    lines = own * heads
    seq_index = lax.axis_index("seq")
    side = lax.rem(seq_index, 2)
    adapter_ids = jnp.arange(HD, dtype=jnp.int32)
    levels = [[2 * level + at for level in range(pairs)] for at in range(2)]
    corners = [
        [head * seqs + 2 * level + at for head in range(groups) for at in (1, 0)]
        for level in range(pairs)
    ]

    def partner(array):
        return lax.ppermute(array, "seq", [(i, i ^ 1) for i in range(seqs)])

    def along_levels(array):
        return lax.all_to_all(array, "seq", 0, 0, tiled=True, axis_index_groups=levels)

    vmem = pltpu.CompilerParams(vmem_limit_bytes=VMEM)
    small = pltpu.CompilerParams(vmem_limit_bytes=16 * 2**20)

    def cost(flops, size):
        return pl.CostEstimate(flops=flops, bytes_accessed=size, transcendentals=0)

    part_shape = jax.ShapeDtypeStruct((pairs, lines + TAIL, width), jnp.bfloat16)
    own_shape = jax.ShapeDtypeStruct((1, lines + TAIL, width), jnp.bfloat16)

    message, own_message = pl.pallas_call(
        pack,
        in_specs=[
            pl.BlockSpec(memory_space=pltpu.VMEM),
            pl.BlockSpec(memory_space=pltpu.SMEM),
        ],
        out_shape=(part_shape, own_shape),
        compiler_params=pltpu.CompilerParams(vmem_limit_bytes=60 * 2**20),
        name="pack",
    )(queries, row_adapter)
    with jax.named_scope("gather_queries"):
        near = along_levels(message)
        far = partner(near)
    doc_len = doc_keys.shape[0]
    slots_here = patch_keys.shape[0]
    tokens = doc_len + slots_here * BLK
    in_vmem = pl.BlockSpec(memory_space=pltpu.VMEM)
    in_smem = pl.BlockSpec(memory_space=pltpu.SMEM)
    local = (
        doc_keys.reshape(doc_len, width),
        doc_values.reshape(doc_len, width),
        jnp.concatenate(
            [
                patch_keys.reshape(slots_here * BLK, width),
                patch_values.reshape(slots_here * BLK, width),
            ],
            0,
        ),
    )
    own_bars, first_bars, second_bars = pl.pallas_call(
        functools.partial(bar, slots_here),
        in_specs=[in_smem] + [in_vmem] * 5,
        out_shape=[jax.ShapeDtypeStruct((tokens // BLK, HD), jnp.float32)] * 3,
        compiler_params=small,
        cost_estimate=cost(10**7, 10**6),
        name="bar",
    )(seq_index.reshape(1), patch_block.reshape(1, -1), patch_slot.reshape(1, -1), *local)

    kept_shapes = (
        jax.ShapeDtypeStruct((pairs, lines, width), jnp.float32),
        jax.ShapeDtypeStruct((pairs, lines), jnp.float32),
    )

    def attend_lines(body, out_shape, messages, first_specs=()):
        return pl.pallas_call(
            body,
            in_specs=list(first_specs) + [in_vmem] * 5,
            out_shape=out_shape,
            compiler_params=vmem,
            cost_estimate=pl.CostEstimate(
                flops=8 * messages * lines * tokens * HD,
                bytes_accessed=4 * tokens * HD + 4 * messages * lines * width,
                transcendentals=messages * lines * tokens,
            ),
            name=body.__name__,
        )

    own_part = attend_lines(attend_own, own_shape, 1)(own_message, *local, own_bars)
    near_part = attend_lines(attend_rest, part_shape, pairs - 1, (in_smem, in_vmem))(
        (seq_index // 2).reshape(1), own_part, near, *local, first_bars
    )
    with jax.named_scope("swap_parts"):
        far_part = partner(near_part)
    mean, logsum = attend_lines(attend_kept, kept_shapes, pairs, (in_vmem,))(
        out_weight, far, *local, second_bars
    )
    merged = pl.pallas_call(
        merge,
        out_shape=part_shape,
        compiler_params=small,
        cost_estimate=cost(10**6, 10**6),
        name="merge",
    )(mean, logsum, far_part)
    late_weight, merged = lax.optimization_barrier((out_weight, merged))
    other_weight = partner(late_weight)
    with jax.named_scope("scatter_rows"):
        parts = along_levels(merged)
    copies = pl.pallas_call(
        combine,
        out_shape=jax.ShapeDtypeStruct((pairs, own, heads * width), jnp.bfloat16),
        compiler_params=small,
        cost_estimate=cost(10**6, 10**6),
        name="combine",
    )(parts)
    with jax.named_scope("gather_attended"):
        attended = along_levels(copies)
    products = pl.pallas_call(
        project,
        in_specs=[in_smem] + [in_vmem] * 3,
        out_shape=jax.ShapeDtypeStruct((pairs, 2, own, out_weight.shape[1]), jnp.bfloat16),
        compiler_params=small,
        cost_estimate=cost(3 * 10**8, 2 * 10**6),
        name="project",
    )(side.reshape(1), attended, out_weight, other_weight)
    with jax.named_scope("sum_heads"):
        shares = lax.all_to_all(
            products.reshape(2 * pairs, own, out_weight.shape[1]),
            ("head", "seq"),
            0,
            0,
            tiled=True,
            axis_index_groups=corners,
        )
        shares = shares.reshape(groups, 2 * own, out_weight.shape[1])
        return pl.pallas_call(
            add_shares,
            out_shape=jax.ShapeDtypeStruct(shares.shape[1:], jnp.float32),
            compiler_params=small,
            cost_estimate=cost(10**6, 10**6),
            name="add_shares",
        )(shares)


def solution(mesh):
    placed = (
        P(("rows", "seq"), "head", None),
        P(("rows", "seq")),
        P("seq", "head", None),
        P("seq", "head", None),
        P("seq", None, "head", None),
        P("seq", None, "head", None),
        P(),
        P(),
        P("head", "seq"),
    )
    return jax.shard_map(
        per_device,
        mesh=mesh,
        in_specs=placed,
        out_specs=P(("rows", "head"), "seq"),
        check_vma=False,
    )
```

```python
import functools
import math

import jax
import jax.numpy as jnp
from jax import lax
from jax.experimental import pallas as pl
from jax.experimental.pallas import tpu as pltpu
from jax.sharding import PartitionSpec as P

BLK = 128
ADAPTERS = 64
PATCHES = 4
HD = 128
RATE = math.log2(math.e) / math.sqrt(HD)
HIDDEN = -1e30
TAIL = 16
SPAN = 1024
OWN_SPAN = 2048
VMEM = 24 * 2**20


def pack(query_ref, adapter_ref, out_ref, own_ref):
    rows, heads, width = query_ref.shape
    query = query_ref[...].astype(jnp.float32)
    line = lax.broadcasted_iota(jnp.int32, (rows, width), 0)
    lane = lax.broadcasted_iota(jnp.int32, (rows, width), 1)
    onehot = jnp.zeros((rows, width), jnp.float32)
    for r in range(rows):
        onehot = jnp.where((line == r) & (lane == adapter_ref[r]), 1.0, onehot)
    lines = [query[:, h, :] for h in range(heads)] + [onehot]
    message = jnp.concatenate(lines, 0).astype(jnp.bfloat16)
    for i in range(out_ref.shape[0]):
        out_ref[i] = message
    own_ref[0] = message


def bar(slots, seq_ref, block_ref, slot_ref, *refs):
    bars_refs = refs[-3:]
    entries = block_ref.shape[1]
    blocks = bars_refs[0].shape[0] - slots
    line = lax.broadcasted_iota(jnp.int32, (blocks + slots, entries), 0)
    named = jnp.where(
        line < blocks,
        jnp.broadcast_to(block_ref[...], line.shape) - seq_ref[0] * blocks,
        jnp.broadcast_to(slot_ref[...], line.shape) - seq_ref[0] * slots + blocks,
    )
    entry = lax.broadcasted_iota(jnp.int32, (entries, HD), 0)
    adapter = lax.broadcasted_iota(jnp.int32, (entries, HD), 1)
    owns = jnp.where(entry // PATCHES == adapter, 1.0, 0.0).astype(jnp.bfloat16)
    hits = jnp.dot(
        jnp.where(named == line, 1.0, 0.0).astype(jnp.bfloat16),
        owns,
        preferred_element_type=jnp.float32,
    )
    is_block = lax.broadcasted_iota(jnp.int32, hits.shape, 0) < blocks
    hidden = jnp.where(is_block, hits, 1.0 - hits) > 0.5
    bars = jnp.where(hidden, HIDDEN, 0.0)
    for bars_ref in bars_refs:
        bars_ref[...] = bars


def store_part(out_ref, i, mean, logsum):
    lines = mean.shape[0]
    line = lax.broadcasted_iota(jnp.int32, (TAIL, lines), 0)
    out_ref[i, :lines, :] = mean.astype(jnp.bfloat16)
    flat = logsum
    first = flat.astype(jnp.bfloat16).astype(jnp.float32)
    second = (flat - first).astype(jnp.bfloat16).astype(jnp.float32)
    third = flat - first - second
    tail = jnp.where(
        line == 0, first, jnp.where(line == 1, second, jnp.where(line == 2, third, 0.0))
    )
    out_ref[i, lines:, :] = tail.astype(jnp.bfloat16)


def local_attention(places, span, msg_ref, doc_ref, doc_values_ref, patches_ref, bars_ref):
    lines = msg_ref.shape[1] - TAIL
    heads = lines // TAIL
    parts = []
    for i in places:
        onehot = msg_ref[i, lines:, :]
        parts.append(
            jnp.concatenate(
                [msg_ref[i, :lines, :], jnp.concatenate([onehot] * heads, 0)], 1
            )
        )
    query = jnp.concatenate(parts, 0)
    ones = jnp.ones((span, HD), jnp.bfloat16)
    peak = accum = None
    bar = 0
    patch_len = patches_ref.shape[0] // 2
    patch_ref = patches_ref.at[pl.ds(0, patch_len)]
    patch_values_ref = patches_ref.at[pl.ds(patch_len, patch_len)]
    for keys_ref, values_ref in ((doc_ref, doc_values_ref), (patch_ref, patch_values_ref)):
        for start in range(0, keys_ref.shape[0], span):
            bars = []
            for _ in range(span // BLK):
                tile = jnp.broadcast_to(bars_ref[bar : bar + 1, :], (TAIL, HD))
                bars += [tile.astype(jnp.bfloat16)] * (BLK // TAIL)
                bar += 1
            keys = jnp.concatenate(
                [keys_ref[start : start + span, :], jnp.concatenate(bars, 0)], 1
            )
            values = jnp.concatenate([values_ref[start : start + span, :], ones], 1)
            scores = lax.dot_general(
                query, keys, (((1,), (1,)), ((), ())), preferred_element_type=jnp.float32
            )
            top = jnp.max(scores, axis=1, keepdims=True)
            if accum is not None:
                top = jnp.maximum(peak, top)
            weights = jnp.exp2((scores - top) * RATE).astype(jnp.bfloat16)
            added = jnp.dot(weights, values, preferred_element_type=jnp.float32)
            accum = added if accum is None else accum * jnp.exp2((peak - top) * RATE) + added
            peak = top
    total = accum[:, HD:]
    mean = accum[:, :HD] / total
    return mean, peak * RATE + jnp.log2(total)


def attend_own(msg_ref, *refs):
    *local, out_ref = refs
    send(range(msg_ref.shape[0]), OWN_SPAN, msg_ref, local, out_ref)


def attend_rest(level_ref, own_ref, msg_ref, *refs):
    *local, out_ref = refs
    count = msg_ref.shape[0]
    out_ref[level_ref[0]] = own_ref[0]
    places = [lax.rem(level_ref[0] + i, count) for i in range(1, count)]
    send(places, SPAN, msg_ref, local, out_ref)


def send(places, span, msg_ref, local, out_ref):
    mean, logsum = local_attention(places, span, msg_ref, *local)
    lines = msg_ref.shape[1] - TAIL
    for i, place in enumerate(places):
        store_part(
            out_ref,
            place,
            mean[i * lines : (i + 1) * lines],
            jnp.transpose(logsum[i * lines : (i + 1) * lines])[:TAIL, :],
        )


def attend_kept(_, msg_ref, *refs):
    *local, mean_ref, logsum_ref = refs
    mean, logsum = local_attention(range(msg_ref.shape[0]), SPAN, msg_ref, *local)
    lines = msg_ref.shape[1] - TAIL
    for i in range(msg_ref.shape[0]):
        mean_ref[i] = mean[i * lines : (i + 1) * lines]
        logsum_ref[i : i + 1, :] = jnp.transpose(logsum[i * lines : (i + 1) * lines])[:1, :]


def columns(flat, lines):
    count = flat.shape[0]
    return jnp.transpose(
        jnp.concatenate([flat, jnp.zeros((lines - count, lines), jnp.float32)], 0)
    )


def merge(mean_ref, logsum_ref, two_ref, out_ref):
    count = two_ref.shape[0]
    lines = two_ref.shape[1] - TAIL
    one = logsum_ref[...]
    two = jnp.sum(two_ref[:, lines:, :].astype(jnp.float32), axis=1)
    top = jnp.maximum(one, two)
    first, second = jnp.exp2(one - top), jnp.exp2(two - top)
    both = first + second
    shares = columns(jnp.concatenate([first / both, second / both], 0), lines)
    logsum = top + jnp.log2(both)
    for i in range(count):
        mean = (
            mean_ref[i] * shares[:, i : i + 1]
            + two_ref[i, :lines, :].astype(jnp.float32) * shares[:, count + i : count + i + 1]
        )
        store_part(out_ref, i, mean, jnp.broadcast_to(logsum[i : i + 1, :], (TAIL, lines)))


def combine(parts_ref, out_ref):
    count = parts_ref.shape[0]
    lines = parts_ref.shape[1] - TAIL
    heads = lines // TAIL
    logsum = jnp.sum(parts_ref[:, lines:, :].astype(jnp.float32), axis=1)
    share = jnp.exp2(logsum - jnp.max(logsum, axis=0, keepdims=True))
    share = columns(share / jnp.sum(share, axis=0, keepdims=True), lines)
    mixed = None
    for i in range(count):
        term = parts_ref[i, :lines, :].astype(jnp.float32) * share[:, i : i + 1]
        mixed = term if mixed is None else mixed + term
    attended = mixed.astype(jnp.bfloat16)
    wide = jnp.concatenate([attended[h * TAIL : (h + 1) * TAIL] for h in range(heads)], 1)
    for i in range(out_ref.shape[0]):
        out_ref[i] = wide


def project(side_ref, rows_ref, own_ref, other_ref, out_ref):
    side = side_ref[0]
    count, own = rows_ref.shape[0], rows_ref.shape[1]
    rows = jnp.concatenate([rows_ref[i] for i in range(count)], 0)
    for weight_ref, place in ((own_ref, 1 - side), (other_ref, side)):
        product = jnp.dot(rows, weight_ref[...], preferred_element_type=jnp.float32)
        product = product.astype(jnp.bfloat16)
        for i in range(count):
            out_ref[i, place] = product[i * own : (i + 1) * own]


def add_shares(shares_ref, out_ref):
    total = shares_ref[0].astype(jnp.float32)
    for i in range(1, shares_ref.shape[0]):
        total = total + shares_ref[i].astype(jnp.float32)
    out_ref[...] = total


def per_device(
    queries,
    row_adapter,
    doc_keys,
    doc_values,
    patch_keys,
    patch_values,
    patch_block,
    patch_slot,
    out_weight,
):
    seqs = lax.axis_size("seq")
    groups = lax.axis_size("head")
    pairs = seqs // 2
    own, heads, width = queries.shape
    lines = own * heads
    seq_index = lax.axis_index("seq")
    side = lax.rem(seq_index, 2)
    adapter_ids = jnp.arange(HD, dtype=jnp.int32)
    levels = [[2 * level + at for level in range(pairs)] for at in range(2)]
    corners = [
        [head * seqs + 2 * level + at for head in range(groups) for at in (1, 0)]
        for level in range(pairs)
    ]

    def partner(array):
        return lax.ppermute(array, "seq", [(i, i ^ 1) for i in range(seqs)])

    def along_levels(array):
        return lax.all_to_all(array, "seq", 0, 0, tiled=True, axis_index_groups=levels)

    vmem = pltpu.CompilerParams(vmem_limit_bytes=VMEM)
    small = pltpu.CompilerParams(vmem_limit_bytes=16 * 2**20)

    def cost(flops, size):
        return pl.CostEstimate(flops=flops, bytes_accessed=size, transcendentals=0)

    part_shape = jax.ShapeDtypeStruct((pairs, lines + TAIL, width), jnp.bfloat16)
    own_shape = jax.ShapeDtypeStruct((1, lines + TAIL, width), jnp.bfloat16)

    message, own_message = pl.pallas_call(
        pack,
        in_specs=[
            pl.BlockSpec(memory_space=pltpu.VMEM),
            pl.BlockSpec(memory_space=pltpu.SMEM),
        ],
        out_shape=(part_shape, own_shape),
        compiler_params=pltpu.CompilerParams(vmem_limit_bytes=60 * 2**20),
        name="pack",
    )(queries, row_adapter)
    with jax.named_scope("gather_queries"):
        near = along_levels(message)
        far = partner(near)
    doc_len = doc_keys.shape[0]
    slots_here = patch_keys.shape[0]
    tokens = doc_len + slots_here * BLK
    in_vmem = pl.BlockSpec(memory_space=pltpu.VMEM)
    in_smem = pl.BlockSpec(memory_space=pltpu.SMEM)
    local = (
        doc_keys.reshape(doc_len, width),
        doc_values.reshape(doc_len, width),
        jnp.concatenate(
            [
                patch_keys.reshape(slots_here * BLK, width),
                patch_values.reshape(slots_here * BLK, width),
            ],
            0,
        ),
    )
    own_bars, first_bars, second_bars = pl.pallas_call(
        functools.partial(bar, slots_here),
        in_specs=[in_smem] + [in_vmem] * 5,
        out_shape=[jax.ShapeDtypeStruct((tokens // BLK, HD), jnp.float32)] * 3,
        compiler_params=small,
        cost_estimate=cost(10**7, 10**6),
        name="bar",
    )(seq_index.reshape(1), patch_block.reshape(1, -1), patch_slot.reshape(1, -1), *local)

    kept_shapes = (
        jax.ShapeDtypeStruct((pairs, lines, width), jnp.float32),
        jax.ShapeDtypeStruct((pairs, lines), jnp.float32),
    )

    def attend_lines(body, out_shape, messages, first_specs=()):
        return pl.pallas_call(
            body,
            in_specs=list(first_specs) + [in_vmem] * 5,
            out_shape=out_shape,
            compiler_params=vmem,
            cost_estimate=pl.CostEstimate(
                flops=8 * messages * lines * tokens * HD,
                bytes_accessed=4 * tokens * HD + 4 * messages * lines * width,
                transcendentals=messages * lines * tokens,
            ),
            name=body.__name__,
        )

    own_part = attend_lines(attend_own, own_shape, 1)(own_message, *local, own_bars)
    near_part = attend_lines(attend_rest, part_shape, pairs - 1, (in_smem, in_vmem))(
        (seq_index // 2).reshape(1), own_part, near, *local, first_bars
    )
    with jax.named_scope("swap_parts"):
        far_part = partner(near_part)
    mean, logsum = attend_lines(attend_kept, kept_shapes, pairs, (in_vmem,))(
        out_weight, far, *local, second_bars
    )
    merged = pl.pallas_call(
        merge,
        out_shape=part_shape,
        compiler_params=small,
        cost_estimate=cost(10**6, 10**6),
        name="merge",
    )(mean, logsum, far_part)
    late_weight, merged = lax.optimization_barrier((out_weight, merged))
    other_weight = partner(late_weight)
    with jax.named_scope("scatter_rows"):
        parts = along_levels(merged)
    copies = pl.pallas_call(
        combine,
        out_shape=jax.ShapeDtypeStruct((pairs, own, heads * width), jnp.bfloat16),
        compiler_params=small,
        cost_estimate=cost(10**6, 10**6),
        name="combine",
    )(parts)
    with jax.named_scope("gather_attended"):
        attended = along_levels(copies)
    products = pl.pallas_call(
        project,
        in_specs=[in_smem] + [in_vmem] * 3,
        out_shape=jax.ShapeDtypeStruct((pairs, 2, own, out_weight.shape[1]), jnp.bfloat16),
        compiler_params=small,
        cost_estimate=cost(3 * 10**8, 2 * 10**6),
        name="project",
    )(side.reshape(1), attended, out_weight, other_weight)
    with jax.named_scope("sum_heads"):
        shares = lax.all_to_all(
            products.reshape(2 * pairs, own, out_weight.shape[1]),
            ("head", "seq"),
            0,
            0,
            tiled=True,
            axis_index_groups=corners,
        )
        shares = shares.reshape(groups, 2 * own, out_weight.shape[1])
        return pl.pallas_call(
            add_shares,
            out_shape=jax.ShapeDtypeStruct(shares.shape[1:], jnp.float32),
            compiler_params=small,
            cost_estimate=cost(10**6, 10**6),
            name="add_shares",
        )(shares)


def solution(mesh):
    placed = (
        P(("rows", "seq"), "head", None),
        P(("rows", "seq")),
        P("seq", "head", None),
        P("seq", "head", None),
        P("seq", None, "head", None),
        P("seq", None, "head", None),
        P(),
        P(),
        P("head", "seq"),
    )
    return jax.shard_map(
        per_device,
        mesh=mesh,
        in_specs=placed,
        out_specs=P(("rows", "head"), "seq"),
        check_vma=False,
    )
```
